128 devices in a mesh: tracer: 4 (over z), sub: 32 (over y, x, core).
Axes of the slice: x: 4, y: 4, z: 4, core: 2. Of those that a mesh axis runs over, the one named last changes fastest.
Arguments:
- factor_lower: float32 [4, 512, 256, 256], P('tracer', 'sub'), may hold values from -1 to 1
- factor_pivot: float32 [4, 512, 256, 256], P('tracer', 'sub'), may hold values from -3 to 3
- factor_upper: float32 [4, 512, 256, 256], P('tracer', 'sub'), may hold values from -1 to 1
- source_pattern: float32 [4, 512, 256], P('tracer', 'sub'), may hold values from -6 to 6
- regions: int32 [512, 256], P('sub'), may hold values from 0 to 599, as said below
- params: float32 [600], replicated, may hold values from -6 to 6
- obs_cells: int32 [4, 8192], P('tracer', 'sub'), may hold values from 0 to 131071, as said below
- obs_values: float32 [4, 8192], P('tracer', 'sub'), may hold values from -6 to 6
Outputs:
- gradient: float32 [600], replicated
- solution: float32 [4, 512, 256], P('tracer', 'sub')
The draws below stay inside these ranges and needn't reach their ends.
Inputs may be any that keep to these rules, and one draw needn't show every extreme that they name: `regions`: A cell of block k carries a region within 3 of k * 600 // 512; the first cell of block 0 carries 0 and the last cell of block 511 carries 600 - 1. `obs_cells`: observations j * 256 to (j + 1) * 256 - 1 of a tracer lie in blocks j * 16 to (j + 1) * 16 - 1; the first two of them sit at the first and the last cell of those blocks. Cells may repeat.
All inputs are finite; a program needn't handle non-finite values.
Results may differ from the reference program's by a relative error of at most 0.0003.
Values sent between devices are 32-bit elements; how exact they have to be, the bound alone decides.
No kernel may reach another device: no remote copies, remote signals or barrier semaphores. Data moves between devices by JAX's collectives and lax.ppermute only.
A program may use at most 192 MiB of HBM per device.

```python
import jax
import jax.numpy as jnp
from jax import lax

B = 256
KB = 16
NP = 600
OBS_DEV = 256
SPECIES_NUMBER = 4
GROUP_NUMBER = 512
NOBS = 8192
N_SUB = 32


def chain_blocks(key, slow_share):
    stochastic_seeds = jax.random.split(key, 7)
    lagging_portion = jax.random.uniform(stochastic_seeds[0], (SPECIES_NUMBER, 1, B)) < slow_share
    slow_rate = jnp.exp(jax.random.uniform(stochastic_seeds[1], (SPECIES_NUMBER, 1, B), jnp.float32, jnp.log(0.1 / GROUP_NUMBER), jnp.log(0.5 / GROUP_NUMBER)))
    fast_rate = jnp.exp(jax.random.uniform(stochastic_seeds[2], (SPECIES_NUMBER, 1, B), jnp.float32, jnp.log(1.0 / 40.0), jnp.log(1.0 / 25.0)))
    rate = jnp.where(lagging_portion, slow_rate, fast_rate)
    device_factor = jnp.exp(jax.random.uniform(stochastic_seeds[3], (SPECIES_NUMBER, N_SUB, B), jnp.float32, jnp.log(0.5), jnp.log(2.0)))
    device_factor = jnp.repeat(device_factor, KB, axis=1)
    emission_positions = jax.random.randint(stochastic_seeds[4], (SPECIES_NUMBER, 2), 0, GROUP_NUMBER)
    emission_pulse = jnp.any(jnp.arange(GROUP_NUMBER)[None, :, None] == emission_positions[:, None, :], axis=-1)
    threshold_entry = jax.random.uniform(stochastic_seeds[5], (SPECIES_NUMBER, GROUP_NUMBER, 1), jnp.float32, 0.5, 0.8)
    kept_selector = jnp.where(emission_pulse[:, :, None] & lagging_portion, threshold_entry, 1.0)
    diagonal = jnp.exp(-rate * device_factor) * kept_selector
    off_part = jnp.clip(jax.random.normal(stochastic_seeds[6], (SPECIES_NUMBER, GROUP_NUMBER, B, B)), -4.0, 4.0) * (0.03 / B ** 0.5)
    identity = jnp.eye(B, dtype=bool)
    return jnp.where(identity, diagonal[:, :, :, None], off_part).astype(jnp.float32)


def draw_factor_lower(key, part):
    key = jax.random.fold_in(key, 3)
    share = 0.5
    return chain_blocks(key, share)


def draw_factor_upper(key, part):
    key = jax.random.fold_in(key, 5)
    share = 0.5
    return chain_blocks(key, share)


def draw_factor_pivot(key, part):
    key = jax.random.fold_in(key, 7)
    key_diag, key_off = jax.random.split(key)
    diagonal = jnp.exp(jax.random.uniform(key_diag, (SPECIES_NUMBER, GROUP_NUMBER, B), jnp.float32, 0.0, jnp.log(3.0)))
    off_part = jnp.clip(jax.random.normal(key_off, (SPECIES_NUMBER, GROUP_NUMBER, B, B)), -4.0, 4.0)
    off_part = off_part * (0.06 / B ** 0.5)
    identity = jnp.eye(B, dtype=bool)
    return jnp.where(identity, diagonal[:, :, :, None], off_part).astype(jnp.float32)


def draw_regions(key, part):
    key = jax.random.fold_in(key, 11)
    center = jnp.arange(GROUP_NUMBER, dtype=jnp.int32) * NP // GROUP_NUMBER
    region = center[:, None] + jax.random.randint(key, (GROUP_NUMBER, B), -3, 4)
    region = jnp.clip(region, 0, NP - 1)
    region = region.at[0, 0].set(0).at[GROUP_NUMBER - 1, B - 1].set(NP - 1)
    return region.astype(jnp.int32)


def draw_obs_cells(key, part):
    key = jax.random.fold_in(key, 13)
    position = jnp.arange(NOBS, dtype=jnp.int32)
    group = position // OBS_DEV
    slot = position % OBS_DEV
    span = KB * B
    offset = jax.random.randint(key, (SPECIES_NUMBER, NOBS), 0, span)
    offset = jnp.where(slot[None, :] == 0, 0, jnp.where(slot[None, :] == 1, span - 1, offset))
    return (group[None, :] * span + offset).astype(jnp.int32)


def steps_of(stream_key, shape, cuts, least, high):
    level, own = 1.0, jax.random.fold_in(stream_key, 6)
    for dim, parts in cuts:
        heights = jnp.exp(jax.random.uniform(jax.random.fold_in(own, dim), (parts,), jnp.float32, least / len(cuts), high / len(cuts)))
        level = level * jnp.repeat(heights, shape[dim] // parts).reshape([-1 if axis == dim else 1 for axis in range(len(shape))])
    return level


def centred(key, extent, width, reach, cuts=(), kind=jnp.bfloat16):
    result = width * jax.random.normal(key, extent, jnp.float32)
    if cuts:
        result = result * steps_of(key, extent, cuts, -0.22, 0.18)
    return jnp.clip(result, -reach, reach).astype(kind)


def setup_inputs(seed: int = 0) -> dict:
    arg_keys = jax.random.split(jax.random.key(seed), 9)
    factor_lower = draw_factor_lower(jax.random.fold_in(arg_keys[8], 71), 0)
    factor_pivot = draw_factor_pivot(jax.random.fold_in(arg_keys[8], 71), 0)
    factor_upper = draw_factor_upper(jax.random.fold_in(arg_keys[8], 71), 0)
    source_pattern = centred(arg_keys[3], (SPECIES_NUMBER, GROUP_NUMBER, B), 1.0, 6.0, ((0, 4), (1, 32)), jnp.float32)
    regions = draw_regions(jax.random.fold_in(arg_keys[8], 71), 0)
    params = centred(arg_keys[5], (NP,), 1.0, 6.0, (), jnp.float32)
    obs_cells = draw_obs_cells(jax.random.fold_in(arg_keys[8], 71), 0)
    obs_values = centred(arg_keys[7], (SPECIES_NUMBER, NOBS), 1.0, 6.0, ((0, 4), (1, 32)), jnp.float32)
    return {"factor_lower": factor_lower, "factor_pivot": factor_pivot, "factor_upper": factor_upper, "source_pattern": source_pattern, "regions": regions, "params": params, "obs_cells": obs_cells, "obs_values": obs_values}


exact_mode = lax.Precision.HIGHEST


def plain_sweep(matrices, terms, reverse):
    def advance(carried, pair):
        matrix, term = pair
        carried = term + jnp.dot(matrix, carried, precision=exact_mode)
        return carried, carried

    start = jnp.zeros(terms.shape[1:], jnp.float32)
    final, states = lax.scan(advance, start, (matrices, terms), reverse=reverse)
    return states


def adjoint_sweep(matrices, terms, reverse):
    def advance(carried, pair):
        matrix, term = pair
        value = term + carried
        return jnp.dot(value, matrix, precision=exact_mode), value

    start = jnp.zeros(terms.shape[1:], jnp.float32)
    final, states = lax.scan(advance, start, (matrices, terms), reverse=reverse)
    return states


def reference(factor_lower, factor_pivot, factor_upper, source_pattern, regions, params, obs_cells, obs_values):
    source_scale = float(GROUP_NUMBER) ** -1.5
    gradient = jnp.zeros((NP,), jnp.float32)
    solutions = []
    for tracer_id in range(SPECIES_NUMBER):
        source = source_scale * source_pattern[tracer_id] * jnp.take(params, regions, axis=0)
        forward = plain_sweep(factor_lower[tracer_id], source, False)
        scaled = jnp.einsum("kij,kj->ki", factor_pivot[tracer_id], forward, precision=exact_mode)
        solution = plain_sweep(factor_upper[tracer_id], scaled, True)
        flat_cells = solution.reshape(-1)
        misfit = jnp.take(flat_cells, obs_cells[tracer_id], axis=0) - obs_values[tracer_id]
        forcing = jnp.zeros((GROUP_NUMBER * B,), jnp.float32).at[obs_cells[tracer_id]].add(misfit).reshape(GROUP_NUMBER, B)
        carried = adjoint_sweep(factor_upper[tracer_id], forcing, False)
        unscaled = jnp.einsum("kji,kj->ki", factor_pivot[tracer_id], carried, precision=exact_mode)
        adjoint = adjoint_sweep(factor_lower[tracer_id], unscaled, True)
        terms = (source_pattern[tracer_id] * adjoint).reshape(-1)
        gradient = gradient + source_scale * jax.ops.segment_sum(terms, regions.reshape(-1), num_segments=NP)
        solutions.append(solution)
    return gradient, jnp.stack(solutions)
```

```python
import functools

import jax
import jax.numpy as jnp
from jax import lax
from jax.experimental import pallas as pl
from jax.experimental.pallas import tpu as pltpu
from jax.sharding import PartitionSpec as P

F32 = jnp.float32
BF16 = jnp.bfloat16
B = 256
AUG = 264
WIN = 32
ROWS = B + WIN
NT = (((1,), (1,)), ((), ()))
NN = (((1,), (0,)), ((), ()))
MIB = 1 << 20
VM = pl.BlockSpec(memory_space=pltpu.VMEM)
SM = pl.BlockSpec(memory_space=pltpu.SMEM)
ANY = pl.BlockSpec(memory_space=pl.ANY)


def split(a):
    high = a.astype(BF16)
    return high, (a - high.astype(F32)).astype(BF16)


def dot3(a, b, dims):
    ah, al = split(a)
    bh, bl = split(b)
    d = functools.partial(lax.dot_general, dimension_numbers=dims, preferred_element_type=F32)
    return d(ah, bh) + (d(ah, bl) + d(al, bh))


def affine(first, second):
    product = dot3(first, second[:B], NN)
    return jnp.concatenate([product[:B], product[B:] + second[B:]], axis=0)


def spread(row):
    return jnp.broadcast_to(row, (128, row.shape[1])).T


def apply(row, mt):
    vb = spread(row)
    return jnp.concatenate(
        [
            jnp.sum(vb * mt[:, :128], axis=0, keepdims=True),
            jnp.sum(vb * mt[:, 128:], axis=0, keepdims=True),
        ],
        axis=1,
    )


def adjoint_column(row, mt):
    acc = mt[:, :128] * row[:, :128] + mt[:, 128:] * row[:, 128:]
    return jnp.sum(acc, axis=1, keepdims=True)


def to_row(column):
    return jnp.broadcast_to(column, (column.shape[0], 128)).T[0:1]


def apply_t(row, mt):
    return to_row(adjoint_column(row, mt))


def place(pos_ref):
    return pos_ref[0], pos_ref[1], pos_ref[2], pos_ref[3]


def row_coords():
    i = lax.broadcasted_iota(jnp.int32, (32, 128), 0)
    return i >> 3, (i >> 1) & 3, i & 1


def scatter_rows(out_ref, pieces):
    for half in range(2):
        total = jnp.zeros((32, 128), F32)
        for mask, row in pieces:
            total = total + jnp.where(mask, row[:, half * 128 : half * 128 + 128], 0.0)
        out_ref[:, half, :] = total


def gather_rows(ref, masks):
    halves = [ref[:, 0, :], ref[:, 1, :]]
    return [
        jnp.concatenate(
            [jnp.sum(jnp.where(m, h, 0.0), axis=0, keepdims=True) for h in halves], axis=1
        )
        for m in masks
    ]


def source_window(k, reg_ref, pat_ref, base, scale):
    rel = reg_ref[pl.ds(k, 1), :] - base
    w = lax.broadcasted_iota(jnp.int32, (WIN, B), 0)
    return jnp.where(w == rel, scale * pat_ref[pl.ds(k, 1), :], 0.0)


def composites_kernel(
    blocks, scale, pos_ref, par_ref, low_hbm, up_hbm, pat_ref, reg_ref,
    own_ref, send_ref, low, up, src, xs, rs, sems
):
    last = blocks - 1

    def copies(k):
        return (
            pltpu.make_async_copy(low_hbm.at[k], low.at[k], sems.at[0, k]),
            pltpu.make_async_copy(up_hbm.at[last - k], up.at[last - k], sems.at[1, k]),
        )

    for k in range(blocks):
        for c in copies(k):
            c.start()
    y, x, core, base = place(pos_ref)
    rel = reg_ref[...] - base
    value = jnp.zeros((blocks, B), F32)
    count = par_ref.shape[0]
    for w in range(WIN):
        value = jnp.where(rel == w, par_ref[jnp.clip(base + w, 0, count - 1)], value)
    src[...] = scale * pat_ref[...] * value
    for c in copies(0):
        c.wait()
    xs[...] = jnp.concatenate([low[0].T, jnp.broadcast_to(src[0:1, :], (8, B))], axis=0)
    rs[...] = up[last].T

    def step(k, carry):
        for c in copies(k):
            c.wait()
        moved = dot3(xs[...], low[k], NT)
        other = dot3(rs[...], up[last - k], NT)
        xs[...] = jnp.concatenate([moved[:B], moved[B:] + src[pl.ds(k, 1), :]], axis=0)
        rs[...] = other
        return carry

    lax.fori_loop(1, blocks, step, 0)
    zero = jnp.zeros((8, B), F32)

    @pl.when(core == 0)
    def _():
        own_ref[...] = xs[...]
        send_ref[:B, :] = rs[...]
        send_ref[B:, :] = zero

    @pl.when(core != 0)
    def _():
        send_ref[...] = xs[...]
        own_ref[:B, :] = rs[...]
        own_ref[B:, :] = zero


def chip_kernel(own_ref, got_ref, out_ref):
    out_ref[...] = affine(own_ref[...], got_ref[...])


def lines_kernel(
    blocks, scale, pos_ref, par_ref, low_hbm, up_hbm, piv_hbm, pat_ref, reg_ref, cells_ref, values_ref, dep_ref,
    y_ref, r_ref, f_ref, cnt_ref, sum_ref, pw_ref, low, up, piv, xs, sems
):
    last = blocks - 1
    y, x, core, base = place(pos_ref)

    def copies(k):
        return (
            pltpu.make_async_copy(low_hbm.at[k], low.at[k], sems.at[0, k]),
            pltpu.make_async_copy(up_hbm.at[last - k], up.at[last - k], sems.at[1, k]),
        )

    def pivot(k):
        return pltpu.make_async_copy(piv_hbm.at[k], piv.at[k], sems.at[2, k])

    for k in range(blocks):
        for c in copies(k):
            c.start()
    for k in range(blocks):
        pivot(last - k).start()

    local = cells_ref[...] - ((y * 4 + x) * 2 + core) * (blocks * B)
    high = local >> 8
    low_part = local & 255
    which = jnp.where(lax.broadcasted_iota(jnp.int32, (blocks, B), 0) == high, 1.0, 0.0)
    slot = jnp.where(lax.broadcasted_iota(jnp.int32, (B, B), 0) == low_part, 1.0, 0.0).astype(BF16)
    weighted = which * values_ref[...]
    v1, rest = weighted.astype(BF16), None
    rest = weighted - v1.astype(F32)
    v2, v3 = split(rest)
    d = functools.partial(lax.dot_general, dimension_numbers=NT, preferred_element_type=F32)
    cnt_ref[...] = d(which.astype(BF16), slot)
    sum_ref[...] = d(v1, slot) + (d(v2, slot) + d(v3, slot))
    wi = lax.broadcasted_iota(jnp.int32, (WIN, 128), 0)
    window = jnp.zeros((WIN, 128), F32)
    count = par_ref.shape[0]
    for w in range(WIN):
        window = jnp.where(wi == w, par_ref[jnp.clip(base + w, 0, count - 1)], window)
    pw_ref[...] = window

    for c in copies(0):
        c.wait()
    xs[0] = jnp.concatenate([low[0].T, source_window(0, reg_ref, pat_ref, base, scale)], axis=0)
    r_ref[last] = up[last].T

    def step(k, carry):
        for c in copies(k):
            c.wait()
        moved = dot3(xs[k - 1], low[k], NT)
        r_ref[last - k] = dot3(r_ref[last - k + 1], up[last - k], NT)
        xs[k] = jnp.concatenate(
            [moved[:B], moved[B:] + source_window(k, reg_ref, pat_ref, base, scale)], axis=0
        )
        return carry

    lax.fori_loop(1, blocks, step, 0)
    f_ref[...] = xs[last, B:, :]
    pivot(last).wait()
    y_ref[last] = dot3(xs[last], piv[last], NT)

    def back(i, carry):
        k = last - i
        pivot(k).wait()
        y_ref[k] = dot3(xs[k], piv[k], NT) + dot3(y_ref[k + 1], up[k], NT)
        return carry

    lax.fori_loop(1, blocks, back, 0)


def line_kernel(pos_ref, own_ref, r1_ref, r2_ref, r3_ref, maps_ref, row_ref, tail_ref):
    y, x, core, base = place(pos_ref)
    p = jnp.where(core == 0, x, 3 - x)
    i = lax.broadcasted_iota(jnp.int32, (AUG, B), 0)
    j = lax.broadcasted_iota(jnp.int32, (AUG, B), 1)
    eye = jnp.where(i == j, 1.0, 0.0)
    r1, r2, r3 = r1_ref[...], r2_ref[...], r3_ref[...]
    maps_ref[0] = jnp.where(p >= 1, r1, eye)
    maps_ref[1] = jnp.where(p >= 2, r2, eye)
    pre = affine(jnp.where(p >= 3, r3, eye), maps_ref[1])
    suf = affine(jnp.where(p <= 2, r3, eye), jnp.where(p <= 1, r2, eye))
    maps_ref[2] = affine(pre, maps_ref[0])
    maps_ref[3] = affine(suf, jnp.where(p <= 0, r1, eye))
    row_ref[...] = affine(affine(maps_ref[2], own_ref[...]), maps_ref[3])
    tail_ref[...] = row_ref[B:, :]


def entering_kernel(own_ref, maps_ref, y1_ref, y2_ref, t3_ref, chip_ref, next_ref):
    inner = y2_ref[B : B + 1, :] + apply(t3_ref[0:1, :], y2_ref[:B, :])
    row = y1_ref[B : B + 1, :] + apply(inner, y1_ref[:B, :])
    chip = maps_ref[2, B : B + 1, :] + apply(row, maps_ref[2, :B, :])
    following = own_ref[B : B + 1, :] + apply(chip, own_ref[:B, :])
    chip_ref[...] = jnp.broadcast_to(chip, (8, B))
    next_ref[...] = jnp.broadcast_to(following, (8, B))


def start_kernel(pos_ref, chip_ref, got_ref, pw_ref, y0_ref, near_ref, suf_ref, in_ref, out_ref):
    my_y, my_x, core, base = place(pos_ref)
    entering = jnp.where(core == 0, chip_ref[0:1, :], got_ref[0:1, :])
    vb = jnp.concatenate([spread(entering), pw_ref[...]], axis=0)
    in_ref[...] = vb
    y0 = y0_ref[0]
    v = jnp.concatenate(
        [
            jnp.sum(vb * y0[:, :128], axis=0, keepdims=True),
            jnp.sum(vb * y0[:, 128:], axis=0, keepdims=True),
        ],
        axis=1,
    )
    z1 = jnp.where(core == 1, apply(v, near_ref[:B, :]), v)
    z2 = apply(z1, suf_ref[0, :B, :])
    ty, tx, tc = row_coords()
    same = ty == my_y
    scatter_rows(
        out_ref,
        [
            (same & (tx == my_x) & (tc < core), v),
            (same & (tx < my_x), z1),
            (ty < my_y, z2),
        ],
    )


def spread_out(out_ref, pos_ref, first, near_ref, maps_ref, d1_ref, d2_ref, leftward):
    my_y, my_x, core, base = place(pos_ref)
    side = 1 if leftward else 0
    g = jnp.where(core == side, apply_t(first, near_ref[:B, :]), first)
    g2 = apply_t(g, maps_ref[0, :B, :])
    g3 = apply_t(g2, maps_ref[1, :B, :])
    h = apply_t(g, maps_ref[2, :B, :])
    h2 = apply_t(h, d1_ref[:B, :])
    h3 = apply_t(h2, d2_ref[:B, :])
    ty, tx, tc = row_coords()
    sign = -1 if leftward else 1
    dy, dx, dc = sign * (ty - my_y), sign * (tx - my_x), sign * (tc - core)
    same = dy == 0
    scatter_rows(
        out_ref,
        [
            (same & (dx == 0) & (dc > 0), first),
            (same & (dx == 1), g),
            (same & (dx == 2), g2),
            (same & (dx == 3), g3),
            (dy == 1, h),
            (dy == 2, h2),
            (dy == 3, h3),
        ],
    )


def collect(got_ref, pos_ref, near_ref, suf, leftward):
    my_y, my_x, core, base = place(pos_ref)
    sy, sx, sc = row_coords()
    same = sy == my_y
    part, mx, my = gather_rows(got_ref, [same & (sx == my_x), same & (sx != my_x), sy != my_y])
    m = mx + apply_t(my, suf)
    side = 0 if leftward else 1
    return part + jnp.where(core == side, apply_t(m, near_ref[:B, :]), m)


def middle_kernel(
    blocks, pos_ref, got_ref, near_ref, maps_ref, d1_ref, d2_ref, in_ref, y_ref, r_ref, cnt_ref, sum_ref,
    sol_ref, out_ref, acc_ref, sb, acc_r
):
    my_y, my_x, core, base = place(pos_ref)
    sy, sx, sc = row_coords()
    same = sy == my_y
    part, t1, t2, t3, y1, y2, y3 = gather_rows(
        got_ref,
        [same & (sx == my_x)]
        + [same & (sx == my_x + j) for j in (1, 2, 3)]
        + [sy == my_y + j for j in (1, 2, 3)],
    )
    yv = y1 + apply(y2 + apply(y3, d2_ref[:B, :]), d1_ref[:B, :])
    xv = t1 + apply(t2 + apply(t3, maps_ref[1, :B, :]), maps_ref[0, :B, :]) + apply(yv, maps_ref[2, :B, :])
    entering = part + jnp.where(core == 0, apply(xv, near_ref[:B, :]), xv)
    sb[...] = spread(entering)
    acc_ref[...] = jnp.zeros((ROWS, 128), F32)
    acc_r[...] = jnp.zeros((B, 128), F32)

    def step(k, carry):
        parts = []
        for half in range(2):
            lanes = slice(half * 128, half * 128 + 128)
            parts.append(
                jnp.sum(in_ref[...] * y_ref[k, :, lanes], axis=0, keepdims=True)
                + jnp.sum(sb[...] * r_ref[k, :, lanes], axis=0, keepdims=True)
            )
        row = jnp.concatenate(parts, axis=1)
        sol_ref[pl.ds(k, 1), :] = row
        forcing = cnt_ref[pl.ds(k, 1), :] * row - sum_ref[pl.ds(k, 1), :]
        left, right = forcing[:, :128], forcing[:, 128:]
        acc_ref[...] += y_ref[k, :, :128] * left + y_ref[k, :, 128:] * right
        acc_r[...] += r_ref[k, :, :128] * left + r_ref[k, :, 128:] * right
        return carry

    lax.fori_loop(0, blocks, step, 0)
    acc_ref[...] = jnp.broadcast_to(jnp.sum(acc_ref[...], axis=1, keepdims=True), (ROWS, 128))
    first = to_row(jnp.sum(acc_r[...], axis=1, keepdims=True))
    spread_out(out_ref, pos_ref, first, near_ref, maps_ref, d1_ref, d2_ref, False)


def return_kernel(
    pos_ref, got_ref, nearu_ref, sufu_ref, acc_ref, y0_ref, nearl_ref, maps_ref, d1_ref, d2_ref, out_ref, gw_ref
):
    c_in = collect(got_ref, pos_ref, nearu_ref, sufu_ref[0, :B, :], False)
    column = acc_ref[:, 0:1] + adjoint_column(c_in, y0_ref[0])
    gw_ref[...] = jnp.broadcast_to(column[B:], (WIN, 128))
    spread_out(out_ref, pos_ref, to_row(column[:B]), nearl_ref, maps_ref, d1_ref, d2_ref, True)


def window_kernel(scale, pos_ref, got_ref, near_ref, suf_ref, gw_ref, f_ref, out_ref):
    my_y, my_x, core, base = place(pos_ref)
    a_in = collect(got_ref, pos_ref, near_ref, suf_ref[0, :B, :], True)
    column = gw_ref[:, 0:1] + adjoint_column(a_in, f_ref[...])
    w = lax.broadcasted_iota(jnp.int32, (WIN, 128), 0)
    lane = lax.broadcasted_iota(jnp.int32, (WIN, 128), 1)
    row = jnp.sum(jnp.where(((base + w) & 127) == lane, column, 0.0), axis=0, keepdims=True)
    out_ref[...] = jnp.broadcast_to(row.reshape(1, 1, 128), out_ref.shape)


def total_kernel(blocks, groups, regions, tracers, got_ref, out_ref):
    total = got_ref[0:32, 0, :]
    for t in range(1, tracers):
        total = total + got_ref[32 * t : 32 * t + 32, 0, :]
    d = lax.broadcasted_iota(jnp.int32, (32, 128), 0)
    lane = lax.broadcasted_iota(jnp.int32, (32, 128), 1)
    base = (d * (blocks * regions)) // groups - 3
    tile = (base + ((lane - base) & 127)) >> 7
    for t in range(out_ref.shape[1] // 128 + 1):
        lo, hi = 128 * t, min(128 * t + 128, out_ref.shape[1])
        if hi > lo:
            row = jnp.sum(jnp.where(tile == t, total, 0.0), axis=0, keepdims=True)
            out_ref[:, lo:hi] = row[:, : hi - lo]


def device(y, x, core):
    return ((y % 4) * 4 + x % 4) * 2 + core


def shards(
    factor_lower, factor_pivot, factor_upper, source_pattern, regions, params, obs_cells, obs_values
):
    low, piv, up = factor_lower[0], factor_pivot[0], factor_upper[0]
    pat = source_pattern[0]
    blocks = low.shape[0]
    tracers = lax.axis_size("tracer")
    groups = blocks * lax.axis_size("sub")
    regions_all = params.shape[0]
    scale = float(groups) ** (-1.5)
    sub = lax.axis_index("sub")
    core = sub & 1
    pos = jnp.stack([sub >> 3, (sub >> 1) & 3, core, (sub * (blocks * regions_all)) // groups - 3])
    pos = pos.astype(jnp.int32)
    left = core == 0

    def shape(*dims):
        return jax.ShapeDtypeStruct(dims, F32)

    def call(kernel, outs, ins, scratch=(), limit=32, flops=0, traffic=0, name=None, grid=None, out_specs=None):
        return pl.pallas_call(
            kernel,
            out_shape=outs,
            in_specs=ins,
            out_specs=out_specs if out_specs is not None else jax.tree.map(lambda _: VM, outs),
            scratch_shapes=list(scratch),
            compiler_params=pltpu.CompilerParams(vmem_limit_bytes=limit * MIB),
            cost_estimate=pl.CostEstimate(flops=flops, bytes_accessed=traffic, transcendentals=0),
            name=name,
            **({"grid": grid} if grid else {}),
        )

    def swap(a):
        return lax.ppermute(a, "sub", [(d, d ^ 1) for d in range(32)])

    def along_x(a, j):
        pairs = [(device(y, x, 0), device(y, x + j, 0)) for y in range(4) for x in range(4)]
        pairs += [(device(y, x, 1), device(y, x - j, 1)) for y in range(4) for x in range(4)]
        return lax.ppermute(a, "sub", pairs)

    def along_y(a, j):
        pairs = [(device(y, x, 0), device(y + j, x, 0)) for y in range(4 - j) for x in range(4)]
        pairs += [(device(y, x, 1), device(y - j, x, 1)) for y in range(j, 4) for x in range(4)]
        return lax.ppermute(a, "sub", pairs)

    def exchange(a):
        return lax.all_to_all(a, "sub", 0, 0)

    block = (blocks, B, B)
    own, send = call(
        functools.partial(composites_kernel, blocks, scale),
        (shape(AUG, B), shape(AUG, B)),
        [SM, SM, ANY, ANY, VM, VM],
        [
            pltpu.VMEM(block, F32), pltpu.VMEM(block, F32), pltpu.VMEM((blocks, B), F32),
            pltpu.VMEM((AUG, B), F32), pltpu.VMEM((B, B), F32), pltpu.SemaphoreType.DMA((2, blocks)),
        ],
        flops=6 * 2 * 16 * B**3, traffic=8 * MIB, name="composites",
    )(pos, params, low, up, pat, regions)
    got = swap(send)
    chip = call(chip_kernel, shape(AUG, B), [VM, VM], flops=6 * B**3, name="chip")(own, got)
    other = swap(own)
    r1, r2, r3 = [along_x(chip, j) for j in (1, 2, 3)]
    yt, rt, ft, cnt, osum, pw = call(
        functools.partial(lines_kernel, blocks, scale),
        (
            shape(blocks, ROWS, B), shape(blocks, B, B), shape(WIN, B), shape(blocks, B), shape(blocks, B),
            shape(WIN, 128),
        ),
        [SM, SM, ANY, ANY, ANY, VM, VM, VM, VM, ANY],
        [
            pltpu.VMEM(block, F32), pltpu.VMEM(block, F32), pltpu.VMEM(block, F32),
            pltpu.VMEM((blocks, ROWS, B), F32), pltpu.SemaphoreType.DMA((3, blocks)),
        ],
        limit=40, flops=6 * 4 * 16 * B**3, traffic=21 * MIB, name="lines",
    )(pos, params, low, up, piv, pat, regions, obs_cells, obs_values, chip)
    maps, row, tail = call(
        line_kernel, (shape(4, AUG, B), shape(AUG, B), shape(8, B)), [SM, VM, VM, VM, VM],
        flops=6 * 6 * B**3, name="line",
    )(pos, chip, r1, r2, r3)
    y1, y2, y3 = along_y(row, 1), along_y(row, 2), along_y(tail, 3)
    maps_o = swap(maps)
    chip_in, following = call(
        entering_kernel, (shape(8, B), shape(8, B)), [VM] * 5, name="entering"
    )(own, maps, y1, y2, y3)
    following = swap(following)
    y1_o, y2_o = swap(y1), swap(y2)
    maps_l, maps_u = jnp.where(left, maps, maps_o), jnp.where(left, maps_o, maps)
    near_u, near_l = jnp.where(left, other, got), jnp.where(left, got, other)
    y1_l, y1_u = jnp.where(left, y1, y1_o), jnp.where(left, y1_o, y1)
    y2_l, y2_u = jnp.where(left, y2, y2_o), jnp.where(left, y2_o, y2)

    def at(shape_, index):
        return pl.BlockSpec(shape_, lambda i, *_: (index, 0, 0))

    def whole(*dims):
        return pl.BlockSpec(dims, lambda i: (0,) * len(dims))

    messages = shape(32, 2, 128)
    mspec = whole(32, 2, 128)
    vb, sent = call(
        start_kernel, (shape(ROWS, 128), messages),
        [SM, whole(8, B), whole(8, B), whole(WIN, 128), at((1, ROWS, B), 0), whole(AUG, B), at((1, AUG, B), 3)],
        name="start", grid=(1,), out_specs=(whole(ROWS, 128), mspec),
    )(pos, chip_in, following, pw, yt, near_u, maps_u)
    got_s = exchange(sent)
    sol, sent, acc = call(
        functools.partial(middle_kernel, blocks),
        (shape(blocks, B), messages, shape(ROWS, 128)),
        [SM] + [VM] * 10,
        [pltpu.VMEM((B, 128), F32), pltpu.VMEM((B, 128), F32)],
        name="middle",
    )(pos, got_s, near_u, maps_u, y1_u, y2_u, vb, yt, rt, cnt, osum)
    got_c = exchange(sent)
    sent, gw = call(
        return_kernel, (messages, shape(WIN, 128)),
        [
            SM, mspec, whole(AUG, B), at((1, AUG, B), 3), whole(ROWS, 128), at((1, ROWS, B), 0),
            whole(AUG, B), whole(4, AUG, B), whole(AUG, B), whole(AUG, B),
        ],
        name="return", grid=(1,), out_specs=(mspec, whole(WIN, 128)),
    )(pos, got_c, near_u, maps_u, acc, yt, near_l, maps_l, y1_l, y2_l)
    got_a = exchange(sent)
    spots = shape(32 * tracers, 1, 128)
    sent = call(
        functools.partial(window_kernel, scale), spots,
        [SM, mspec, whole(AUG, B), at((1, AUG, B), 3), whole(WIN, 128), whole(WIN, B)],
        name="window", grid=(1,), out_specs=whole(32 * tracers, 1, 128),
    )(pos, got_a, near_l, maps_l, gw, ft)
    spread_windows = lax.all_to_all(sent, ("tracer", "sub"), 0, 0)
    gradient = call(
        functools.partial(total_kernel, blocks, groups, regions_all, tracers), shape(1, regions_all), [VM],
        name="total",
    )(spread_windows)
    return (gradient.reshape(regions_all), sol[None])


def solution(mesh):
    return jax.shard_map(
        shards,
        mesh=mesh,
        in_specs=(
            P("tracer", "sub", None, None),
            P("tracer", "sub", None, None),
            P("tracer", "sub", None, None),
            P("tracer", "sub", None),
            P("sub", None),
            P(),
            P("tracer", "sub"),
            P("tracer", "sub"),
        ),
        out_specs=(P(), P("tracer", "sub", None)),
        check_vma=False,
    )
```

```python
import functools

import jax
import jax.numpy as jnp
from jax import lax
from jax.experimental import pallas as pl
from jax.experimental.pallas import tpu as pltpu
from jax.sharding import PartitionSpec as P

F32 = jnp.float32
BF16 = jnp.bfloat16
B = 256
AUG = 264
WIN = 32
ROWS = B + WIN
NT = (((1,), (1,)), ((), ()))
NN = (((1,), (0,)), ((), ()))
MIB = 1 << 20
UNROLL = True
VM = pl.BlockSpec(memory_space=pltpu.VMEM)
SM = pl.BlockSpec(memory_space=pltpu.SMEM)
ANY = pl.BlockSpec(memory_space=pl.ANY)
HBM = pl.BlockSpec(memory_space=pltpu.HBM)


def split(a):
    high = a.astype(BF16)
    return high, (a - high.astype(F32)).astype(BF16)


def dot3(a, b, dims):
    ah, al = split(a)
    bh, bl = split(b)
    return lax.dot_general(
        jnp.concatenate([ah, ah, al], axis=1),
        jnp.concatenate([bh, bl, bh], axis=dims[0][1][0]),
        dims,
        preferred_element_type=F32,
    )


def unit():
    i = lax.broadcasted_iota(jnp.int32, (B, B), 0)
    return jnp.where(i == lax.broadcasted_iota(jnp.int32, (B, B), 1), 1.0, 0.0)


def advance(a, b, dims=NT):
    return a + dot3(a, b - unit(), dims)


def affine(first, second):
    product = advance(first, second[:B], NN)
    return jnp.concatenate([product[:B], product[B:] + second[B:]], axis=0)


def spread(row):
    return jnp.broadcast_to(row, (128, row.shape[1])).T


def apply(row, mt):
    vb = spread(row)
    return jnp.concatenate(
        [
            jnp.sum(vb * mt[:, :128], axis=0, keepdims=True),
            jnp.sum(vb * mt[:, 128:], axis=0, keepdims=True),
        ],
        axis=1,
    )


def adjoint_column(row, mt):
    acc = mt[:, :128] * row[:, :128] + mt[:, 128:] * row[:, 128:]
    return jnp.sum(acc, axis=1, keepdims=True)


def to_row(column):
    return jnp.broadcast_to(column, (column.shape[0], 128)).T[0:1]


def apply_t(row, mt):
    return to_row(adjoint_column(row, mt))


def place():
    sub = lax.axis_index("sub")
    return sub >> 3, (sub >> 1) & 3, sub & 1


def window_base(blocks, regions):
    groups = blocks * lax.axis_size("sub")
    return (lax.axis_index("sub") * (blocks * regions)) // groups - 3


def row_coords():
    i = lax.broadcasted_iota(jnp.int32, (32, 128), 0)
    return i >> 3, (i >> 1) & 3, i & 1


def scatter_rows(out_ref, pieces):
    for half in range(2):
        total = jnp.zeros((32, 128), F32)
        for mask, row in pieces:
            total = total + jnp.where(mask, row[:, half * 128 : half * 128 + 128], 0.0)
        out_ref[:, half, :] = total


def gather_rows(ref, masks):
    halves = [ref[:, 0, :], ref[:, 1, :]]
    return [
        jnp.concatenate(
            [jnp.sum(jnp.where(m, h, 0.0), axis=0, keepdims=True) for h in halves], axis=1
        )
        for m in masks
    ]


def source_window(k, reg_ref, pat_ref, base, scale):
    rel = reg_ref[pl.ds(k, 1), :] - base
    w = lax.broadcasted_iota(jnp.int32, (WIN, B), 0)
    return jnp.where(w == rel, scale * pat_ref[pl.ds(k, 1), :], 0.0)


def composites_kernel(
    blocks, scale, low_hbm, up_hbm, pat_hbm, reg_hbm, par_hbm,
    own_ref, send_ref, low, up, pat, reg, par, src, xa, xb, ra, rb, sems, small
):
    half = blocks // 2
    last = blocks - 1

    def copies(k):
        return (
            pltpu.make_async_copy(low_hbm.at[k], low.at[k], sems.at[0, k]),
            pltpu.make_async_copy(up_hbm.at[last - k], up.at[last - k], sems.at[1, k]),
        )

    extras = (
        pltpu.make_async_copy(par_hbm, par, small.at[0]),
        pltpu.make_async_copy(reg_hbm, reg, small.at[1]),
        pltpu.make_async_copy(pat_hbm, pat, small.at[2]),
    )
    for c in extras:
        c.start()
    for k in range(half):
        for c in copies(k) + copies(k + half):
            c.start()
    y, x, core = place()
    count = par.shape[0]
    base = window_base(blocks, count)
    for c in extras:
        c.wait()
    rel = reg[...] - base
    value = jnp.zeros((blocks, B), F32)
    for w in range(WIN):
        value = jnp.where(rel == w, par[jnp.clip(base + w, 0, count - 1)], value)
    src[...] = scale * pat[...] * value
    for c in copies(0) + copies(half):
        c.wait()
    xa[...] = jnp.concatenate([low[0].T, jnp.broadcast_to(src[0:1, :], (8, B))], axis=0)
    xb[...] = jnp.concatenate([low[half].T, jnp.broadcast_to(src[half : half + 1, :], (8, B))], axis=0)
    ra[...] = up[last].T
    rb[...] = up[last - half].T

    def step(k, carry):
        for c in copies(k) + copies(k + half):
            c.wait()
        a = advance(xa[...], low[k])
        b = advance(xb[...], low[k + half])
        c = advance(ra[...], up[last - k])
        d = advance(rb[...], up[last - half - k])
        xa[:B, :] = a[:B]
        xa[B:, :] = a[B:] + src[pl.ds(k, 1), :]
        xb[:B, :] = b[:B]
        xb[B:, :] = b[B:] + src[pl.ds(k + half, 1), :]
        ra[...] = c
        rb[...] = d
        return carry

    lax.fori_loop(1, half, step, 0, unroll=UNROLL)
    xs = affine(xa[...], xb[...])
    rs = advance(ra[...], rb[...], NN)
    zero = jnp.zeros((8, B), F32)

    @pl.when(core == 0)
    def _():
        own_ref[...] = xs
        send_ref[:B, :] = rs
        send_ref[B:, :] = zero

    @pl.when(core != 0)
    def _():
        send_ref[...] = xs
        own_ref[:B, :] = rs
        own_ref[B:, :] = zero


def chip_kernel(own_ref, got_ref, out_ref):
    out_ref[...] = affine(own_ref[...], got_ref[...])


def prefixes_kernel(
    blocks, scale, low_hbm, up_hbm, pat_ref, reg_ref, par_ref, cells_ref, values_ref, dep_ref,
    x_ref, r_ref, cnt_ref, sum_ref, pw_ref, low, up, sems
):
    last = blocks - 1
    y, x, core = place()

    def copies(k):
        return (
            pltpu.make_async_copy(low_hbm.at[k], low.at[k], sems.at[0, k]),
            pltpu.make_async_copy(up_hbm.at[last - k], up.at[last - k], sems.at[1, k]),
        )

    for k in range(blocks):
        for c in copies(k):
            c.start()
    count = par_ref.shape[0]
    base = window_base(blocks, count)
    local = cells_ref[...] - ((y * 4 + x) * 2 + core) * (blocks * B)
    high = local >> 8
    low_part = local & 255
    which = jnp.where(lax.broadcasted_iota(jnp.int32, (blocks, B), 0) == high, 1.0, 0.0)
    slot = jnp.where(lax.broadcasted_iota(jnp.int32, (B, B), 0) == low_part, 1.0, 0.0).astype(BF16)
    weighted = which * values_ref[...]
    v1 = weighted.astype(BF16)
    v2, v3 = split(weighted - v1.astype(F32))
    d = functools.partial(lax.dot_general, dimension_numbers=NT, preferred_element_type=F32)
    cnt_ref[...] = d(which.astype(BF16), slot)
    sum_ref[...] = d(v1, slot) + (d(v2, slot) + d(v3, slot))
    wi = lax.broadcasted_iota(jnp.int32, (WIN, 128), 0)
    window = jnp.zeros((WIN, 128), F32)
    for w in range(WIN):
        window = jnp.where(wi == w, par_ref[jnp.clip(base + w, 0, count - 1)], window)
    pw_ref[...] = window

    for c in copies(0):
        c.wait()
    x_ref[0] = jnp.concatenate([low[0].T, source_window(0, reg_ref, pat_ref, base, scale)], axis=0)
    r_ref[last] = up[last].T

    def step(k, carry):
        for c in copies(k):
            c.wait()
        moved = advance(x_ref[k - 1], low[k])
        r_ref[last - k] = advance(r_ref[last - k + 1], up[last - k])
        x_ref[k, :B, :] = moved[:B]
        x_ref[k, B:, :] = moved[B:] + source_window(k, reg_ref, pat_ref, base, scale)
        return carry

    lax.fori_loop(1, blocks, step, 0, unroll=UNROLL)


def lines_kernel(blocks, up_hbm, piv_hbm, x_ref, dep_ref, y_ref, token_ref, up, piv, sems):
    last = blocks - 1

    def copies(k):
        return (
            pltpu.make_async_copy(up_hbm.at[k], up.at[k], sems.at[0, k]),
            pltpu.make_async_copy(piv_hbm.at[k], piv.at[k], sems.at[1, k]),
        )

    for i in range(blocks):
        for c in copies(last - i):
            c.start()
    for c in copies(last):
        c.wait()
    y_ref[last] = dot3(x_ref[last], piv[last], NT)

    def back(i, carry):
        k = last - i
        for c in copies(k):
            c.wait()
        y_ref[k] = dot3(x_ref[k], piv[k], NT) + advance(y_ref[k + 1], up[k])
        return carry

    lax.fori_loop(1, blocks, back, 0, unroll=UNROLL)
    token_ref[...] = jnp.zeros((8, 128), F32)


def line_kernel(own_ref, r1_ref, r2_ref, r3_ref, dep_ref, maps_ref, row_ref, tail_ref):
    y, x, core = place()
    p = jnp.where(core == 0, x, 3 - x)
    i = lax.broadcasted_iota(jnp.int32, (AUG, B), 0)
    j = lax.broadcasted_iota(jnp.int32, (AUG, B), 1)
    eye = jnp.where(i == j, 1.0, 0.0)
    r1, r2, r3 = r1_ref[...], r2_ref[...], r3_ref[...]
    maps_ref[0] = jnp.where(p >= 1, r1, eye)
    maps_ref[1] = jnp.where(p >= 2, r2, eye)
    pre = affine(jnp.where(p >= 3, r3, eye), maps_ref[1])
    suf = affine(jnp.where(p <= 2, r3, eye), jnp.where(p <= 1, r2, eye))
    maps_ref[2] = affine(pre, maps_ref[0])
    maps_ref[3] = affine(suf, jnp.where(p <= 0, r1, eye))
    row_ref[...] = affine(affine(maps_ref[2], own_ref[...]), maps_ref[3])
    tail_ref[...] = row_ref[B:, :]


def entering_kernel(own_ref, maps_ref, y1_ref, y2_ref, t3_ref, dep_ref, chip_ref, next_ref):
    y, x, core = place()
    t1 = jnp.where(y >= 1, y1_ref[B : B + 1, :], 0.0)
    t2 = jnp.where(y >= 2, y2_ref[B : B + 1, :], 0.0)
    t3 = jnp.where(y >= 3, t3_ref[0:1, :], 0.0)
    row = t1 + apply(t2 + apply(t3, y2_ref[:B, :]), y1_ref[:B, :])
    chip = maps_ref[2, B : B + 1, :] + apply(row, maps_ref[2, :B, :])
    following = own_ref[B : B + 1, :] + apply(chip, own_ref[:B, :])
    chip_ref[...] = jnp.broadcast_to(chip, (8, B))
    next_ref[...] = jnp.broadcast_to(following, (8, B))


def start_kernel(chip_ref, got_ref, pw_ref, y_ref, near0_ref, near1_ref, maps_ref, mapso_ref, dep1_ref, dep2_ref, in_ref, out_ref):
    my_y, my_x, core = place()
    entering = jnp.where(core == 0, chip_ref[0:1, :], got_ref[0:1, :])
    vb = jnp.concatenate([spread(entering), pw_ref[...]], axis=0)
    in_ref[...] = vb
    v = jnp.concatenate(
        [
            jnp.sum(vb * y_ref[0, :, :128], axis=0, keepdims=True),
            jnp.sum(vb * y_ref[0, :, 128:], axis=0, keepdims=True),
        ],
        axis=1,
    )
    z1 = jnp.where(core == 1, apply(v, near1_ref[:B, :]), v)
    z2 = apply(z1, jnp.where(core == 1, maps_ref[3, :B, :], mapso_ref[3, :B, :]))
    ty, tx, tc = row_coords()
    same = ty == my_y
    scatter_rows(
        out_ref,
        [
            (same & (tx == my_x) & (tc < core), v),
            (same & (tx < my_x), z1),
            (ty < my_y, z2),
        ],
    )


class Maps:
    def __init__(self, core, side, near, maps, steps):
        self.mine = core == side
        self.near_refs, self.map_refs, self.step_refs = near, maps, steps

    def near(self):
        return jnp.where(self.mine, self.near_refs[0][:B, :], self.near_refs[1][:B, :])

    def line(self, i):
        return jnp.where(self.mine, self.map_refs[0][i, :B, :], self.map_refs[1][i, :B, :])

    def step(self, j):
        mine, other = self.step_refs[j - 1]
        return jnp.where(self.mine, mine[:B, :], other[:B, :])


def spread_out(out_ref, first, m, leftward):
    my_y, my_x, core = place()
    side = 1 if leftward else 0
    g = jnp.where(core == side, apply_t(first, m.near()), first)
    g2 = apply_t(g, m.line(0))
    g3 = apply_t(g2, m.line(1))
    h = apply_t(g, m.line(2))
    h2 = apply_t(h, m.step(1))
    h3 = apply_t(h2, m.step(2))
    ty, tx, tc = row_coords()
    sign = -1 if leftward else 1
    dy, dx, dc = sign * (ty - my_y), sign * (tx - my_x), sign * (tc - core)
    same = dy == 0
    scatter_rows(
        out_ref,
        [
            (same & (dx == 0) & (dc > 0), first),
            (same & (dx == 1), g),
            (same & (dx == 2), g2),
            (same & (dx == 3), g3),
            (dy == 1, h),
            (dy == 2, h2),
            (dy == 3, h3),
        ],
    )


def collect(got_ref, m, leftward):
    my_y, my_x, core = place()
    sy, sx, sc = row_coords()
    same = sy == my_y
    part, mx, my = gather_rows(got_ref, [same & (sx == my_x), same & (sx != my_x), sy != my_y])
    total = mx + apply_t(my, m.line(3))
    side = 0 if leftward else 1
    return part + jnp.where(core == side, apply_t(total, m.near()), total)


def middle_kernel(
    blocks, got_ref, got0_ref, other_ref, maps_ref, mapso_ref, y1_ref, y1o_ref, y2_ref, y2o_ref,
    in_ref, y_ref, r_ref, cnt_ref, sum_ref, sol_ref, out_ref, acc_ref, sb, acc_r
):
    my_y, my_x, core = place()
    m = Maps(core, 1, (got0_ref, other_ref), (maps_ref, mapso_ref), ((y1_ref, y1o_ref), (y2_ref, y2o_ref)))
    sy, sx, sc = row_coords()
    same = sy == my_y
    part, t1, t2, t3, y1, y2, y3 = gather_rows(
        got_ref,
        [same & (sx == my_x)]
        + [same & (sx == my_x + j) for j in (1, 2, 3)]
        + [sy == my_y + j for j in (1, 2, 3)],
    )
    yv = y1 + apply(y2 + apply(y3, m.step(2)), m.step(1))
    xv = t1 + apply(t2 + apply(t3, m.line(1)), m.line(0)) + apply(yv, m.line(2))
    entering = part + jnp.where(core == 0, apply(xv, m.near()), xv)
    sb[...] = spread(entering)
    acc_ref[...] = jnp.zeros((ROWS, 128), F32)
    acc_r[...] = jnp.zeros((B, 128), F32)

    for k in range(blocks):
        vb, wb = in_ref[...], sb[...]
        row = jnp.concatenate(
            [
                jnp.sum(vb * y_ref[k, :, half], axis=0, keepdims=True)
                + jnp.sum(wb * r_ref[k, :, half], axis=0, keepdims=True)
                for half in (slice(0, 128), slice(128, 256))
            ],
            axis=1,
        )
        sol_ref[k : k + 1, :] = row
        forcing = cnt_ref[k : k + 1, :] * row - sum_ref[k : k + 1, :]
        left, right = forcing[:, :128], forcing[:, 128:]
        acc_ref[...] += y_ref[k, :, :128] * left + y_ref[k, :, 128:] * right
        acc_r[...] += r_ref[k, :, :128] * left + r_ref[k, :, 128:] * right

    acc_ref[...] = jnp.broadcast_to(jnp.sum(acc_ref[...], axis=1, keepdims=True), (ROWS, 128))
    first = to_row(jnp.sum(acc_r[...], axis=1, keepdims=True))
    spread_out(out_ref, first, m, False)


def return_kernel(
    got_ref, got0_ref, other_ref, maps_ref, mapso_ref, y1_ref, y1o_ref, y2_ref, y2o_ref, acc_ref, y_ref,
    out_ref, gw_ref
):
    core = place()[2]
    upper = Maps(core, 1, (got0_ref, other_ref), (maps_ref, mapso_ref), None)
    lower = Maps(core, 0, (got0_ref, other_ref), (maps_ref, mapso_ref), ((y1_ref, y1o_ref), (y2_ref, y2o_ref)))
    c_in = collect(got_ref, upper, False)
    column = acc_ref[:, 0:1] + adjoint_column(c_in, y_ref[0])
    gw_ref[...] = jnp.broadcast_to(column[B:], (WIN, 128))
    spread_out(out_ref, to_row(column[:B]), lower, True)


def window_kernel(blocks, regions, got_ref, got0_ref, other_ref, maps_ref, mapso_ref, gw_ref, x_ref, out_ref):
    core = place()[2]
    base = window_base(blocks, regions)
    lower = Maps(core, 0, (got0_ref, other_ref), (maps_ref, mapso_ref), None)
    a_in = collect(got_ref, lower, True)
    column = gw_ref[:, 0:1] + adjoint_column(a_in, x_ref[blocks - 1, B:, :])
    w = lax.broadcasted_iota(jnp.int32, (WIN, 128), 0)
    lane = lax.broadcasted_iota(jnp.int32, (WIN, 128), 1)
    row = jnp.sum(jnp.where(((base + w) & 127) == lane, column, 0.0), axis=0, keepdims=True)
    out_ref[...] = jnp.broadcast_to(row.reshape(1, 1, 128), out_ref.shape)


def total_kernel(blocks, groups, regions, tracers, got_ref, out_ref):
    total = got_ref[0:32, 0, :]
    for t in range(1, tracers):
        total = total + got_ref[32 * t : 32 * t + 32, 0, :]
    d = lax.broadcasted_iota(jnp.int32, (32, 128), 0)
    lane = lax.broadcasted_iota(jnp.int32, (32, 128), 1)
    base = (d * (blocks * regions)) // groups - 3
    tile = (base + ((lane - base) & 127)) >> 7
    for t in range(out_ref.shape[1] // 128 + 1):
        lo, hi = 128 * t, min(128 * t + 128, out_ref.shape[1])
        if hi > lo:
            row = jnp.sum(jnp.where(tile == t, total, 0.0), axis=0, keepdims=True)
            out_ref[:, lo:hi] = row[:, : hi - lo]


def device(y, x, core):
    return ((y % 4) * 4 + x % 4) * 2 + core


def shards(
    factor_lower, factor_pivot, factor_upper, source_pattern, regions, params, obs_cells, obs_values
):
    low, piv, up = factor_lower[0], factor_pivot[0], factor_upper[0]
    pat = source_pattern[0]
    blocks = low.shape[0]
    tracers = lax.axis_size("tracer")
    groups = blocks * lax.axis_size("sub")
    regions_all = params.shape[0]
    scale = float(groups) ** (-1.5)
    def shape(*dims):
        return jax.ShapeDtypeStruct(dims, F32)

    def near(*dims):
        return pltpu.VMEM(dims, F32)

    def far(*arrays):
        return [pltpu.with_memory_space_constraint(a, pltpu.HBM) for a in arrays]

    def call(kernel, outs, ins, scratch=(), limit=8, flops=0, traffic=0, name=None):
        return pl.pallas_call(
            kernel,
            out_shape=outs,
            in_specs=ins,
            out_specs=jax.tree.map(lambda _: VM, outs),
            scratch_shapes=list(scratch),
            compiler_params=pltpu.CompilerParams(vmem_limit_bytes=limit * MIB),
            cost_estimate=pl.CostEstimate(flops=flops, bytes_accessed=traffic, transcendentals=0),
            name=name,
        )

    def swap(a):
        return lax.ppermute(a, "sub", [(d, d ^ 1) for d in range(32)])

    def along_x(a, j):
        pairs = [(device(y, x, 0), device(y, x + j, 0)) for y in range(4) for x in range(4)]
        pairs += [(device(y, x, 1), device(y, x - j, 1)) for y in range(4) for x in range(4)]
        return lax.ppermute(a, "sub", pairs)

    def along_y(a, j):
        pairs = [(device(y, x, 0), device(y + j, x, 0)) for y in range(4) for x in range(4)]
        pairs += [(device(y, x, 1), device(y - j, x, 1)) for y in range(4) for x in range(4)]
        return lax.ppermute(a, "sub", pairs)

    def exchange(a):
        return lax.all_to_all(a, "sub", 0, 0)

    block = (blocks, B, B)
    own, send = call(
        functools.partial(composites_kernel, blocks, scale),
        (shape(AUG, B), shape(AUG, B)),
        [HBM] * 5,
        [
            pltpu.VMEM(block, F32), pltpu.VMEM(block, F32), pltpu.VMEM((blocks, B), F32),
            pltpu.VMEM((blocks, B), jnp.int32), pltpu.SMEM((regions_all,), F32), pltpu.VMEM((blocks, B), F32),
            pltpu.VMEM((AUG, B), F32), pltpu.VMEM((AUG, B), F32), pltpu.VMEM((B, B), F32), pltpu.VMEM((B, B), F32),
            pltpu.SemaphoreType.DMA((2, blocks)), pltpu.SemaphoreType.DMA((3,)),
        ],
        limit=20, flops=6 * 2 * 16 * B**3, traffic=8 * MIB, name="composites",
    )(*far(low, up, pat, regions, params))
    got = swap(send)
    chip = call(chip_kernel, shape(AUG, B), [VM, VM], flops=6 * B**3, name="chip")(own, got)
    r1, r2, r3 = [along_x(chip, j) for j in (1, 2, 3)]
    other = swap(own)
    xt, rt, cnt, osum, pw = call(
        functools.partial(prefixes_kernel, blocks, scale),
        (near(blocks, ROWS, B), near(blocks, B, B), near(blocks, B), near(blocks, B), near(WIN, 128)),
        [HBM, HBM, VM, VM, SM, VM, VM, ANY],
        [pltpu.VMEM(block, F32), pltpu.VMEM(block, F32), pltpu.SemaphoreType.DMA((2, blocks))],
        limit=14, flops=6 * 2 * 16 * B**3, traffic=8 * MIB, name="prefixes",
    )(*far(low, up), pat, regions, params, obs_cells, obs_values, chip)
    maps, row, tail = call(
        line_kernel, (shape(4, AUG, B), shape(AUG, B), shape(8, B)), [VM, VM, VM, VM, ANY],
        flops=6 * 6 * B**3, name="line",
    )(chip, r1, r2, r3, cnt)
    y1, y2, y3 = along_y(row, 1), along_y(row, 2), along_y(tail, 3)
    maps_o = swap(maps)
    yt, token = call(
        functools.partial(lines_kernel, blocks),
        (near(blocks, ROWS, B), near(8, 128)),
        [HBM, HBM, VM, ANY],
        [pltpu.VMEM(block, F32), pltpu.VMEM(block, F32), pltpu.SemaphoreType.DMA((2, blocks))],
        limit=14, flops=6 * 2 * 16 * B**3, traffic=8 * MIB, name="lines",
    )(*far(up, piv), xt, tail)
    chip_in, following = call(
        entering_kernel, (shape(8, B), shape(8, B)), [VM] * 5 + [ANY], name="entering"
    )(own, maps, y1, y2, y3, token)
    following = swap(following)
    y1_o, y2_o = [swap(a) for a in lax.optimization_barrier((y1, y2, token))[:2]]
    messages = shape(32, 2, 128)
    vb, sent = call(start_kernel, (near(ROWS, 128), messages), [VM] * 8 + [ANY] * 2, name="start")(
        chip_in, following, pw, yt, other, got, maps, maps_o, y1_o, y2_o
    )
    got_s = exchange(sent)
    sol, sent, acc = call(
        functools.partial(middle_kernel, blocks),
        (shape(blocks, B), messages, near(ROWS, 128)),
        [VM] * 14,
        [pltpu.VMEM((B, 128), F32), pltpu.VMEM((B, 128), F32)],
        name="middle",
    )(got_s, got, other, maps, maps_o, y1, y1_o, y2, y2_o, vb, yt, rt, cnt, osum)
    got_c = exchange(sent)
    sent, gw = call(return_kernel, (messages, near(WIN, 128)), [VM] * 11, name="return")(
        got_c, got, other, maps, maps_o, y1, y1_o, y2, y2_o, acc, yt
    )
    got_a = exchange(sent)
    sent = call(
        functools.partial(window_kernel, blocks, regions_all), shape(32 * tracers, 1, 128), [VM] * 7, name="window"
    )(got_a, got, other, maps, maps_o, gw, xt)
    spread_windows = lax.all_to_all(sent, ("tracer", "sub"), 0, 0)
    gradient = call(
        functools.partial(total_kernel, blocks, groups, regions_all, tracers), shape(1, regions_all), [VM],
        name="total",
    )(spread_windows)
    return (gradient.reshape(regions_all), sol[None])


def solution(mesh):
    return jax.shard_map(
        shards,
        mesh=mesh,
        in_specs=(
            P("tracer", "sub", None, None),
            P("tracer", "sub", None, None),
            P("tracer", "sub", None, None),
            P("tracer", "sub", None),
            P("sub", None),
            P(),
            P("tracer", "sub"),
            P("tracer", "sub"),
        ),
        out_specs=(P(), P("tracer", "sub", None)),
        check_vma=False,
    )
```

```python
import functools

import jax
import jax.numpy as jnp
from jax import lax
from jax.experimental import pallas as pl
from jax.experimental.pallas import tpu as pltpu
from jax.sharding import PartitionSpec as P

F32 = jnp.float32
BF16 = jnp.bfloat16
B = 256
AUG = 264
WIN = 32
ROWS = B + WIN
NT = (((1,), (1,)), ((), ()))
NN = (((1,), (0,)), ((), ()))
MIB = 1 << 20
PARTS = 4
DEPTH = 2
VM = pl.BlockSpec(memory_space=pltpu.VMEM)
SM = pl.BlockSpec(memory_space=pltpu.SMEM)
ANY = pl.BlockSpec(memory_space=pl.ANY)
HBM = pl.BlockSpec(memory_space=pltpu.HBM)


def split(a):
    high = a.astype(BF16)
    return high, (a - high.astype(F32)).astype(BF16)


def dot3(a, b, dims):
    ah, al = split(a)
    bh, bl = split(b)
    return lax.dot_general(
        jnp.concatenate([ah, ah, al], axis=1),
        jnp.concatenate([bh, bl, bh], axis=dims[0][1][0]),
        dims,
        preferred_element_type=F32,
    )


def less_unit(b):
    i = lax.broadcasted_iota(jnp.int32, (128, 128), 0)
    unit = jnp.where(i == lax.broadcasted_iota(jnp.int32, (128, 128), 1), 1.0, 0.0)
    top = jnp.concatenate([b[:128, :128] - unit, b[:128, 128:]], axis=1)
    return jnp.concatenate([top, jnp.concatenate([b[128:, :128], b[128:, 128:] - unit], axis=1)], axis=0)


def advance(a, b, dims=NT):
    return a + dot3(a, less_unit(b), dims)


def affine(first, second):
    product = advance(first, second[:B], NN)
    return jnp.concatenate([product[:B], product[B:] + second[B:]], axis=0)


def spread(row):
    return jnp.broadcast_to(row, (128, row.shape[1])).T


def apply(row, mt):
    vb = spread(row)
    return jnp.concatenate(
        [
            jnp.sum(vb * mt[:, :128], axis=0, keepdims=True),
            jnp.sum(vb * mt[:, 128:], axis=0, keepdims=True),
        ],
        axis=1,
    )


def adjoint_column(row, mt):
    acc = mt[:, :128] * row[:, :128] + mt[:, 128:] * row[:, 128:]
    return jnp.sum(acc, axis=1, keepdims=True)


def to_row(column):
    return jnp.broadcast_to(column, (column.shape[0], 128)).T[0:1]


def apply_t(row, mt):
    return to_row(adjoint_column(row, mt))


def place():
    sub = lax.axis_index("sub")
    return sub >> 3, (sub >> 1) & 3, sub & 1


def window_base(blocks, regions):
    groups = blocks * lax.axis_size("sub")
    return (lax.axis_index("sub") * (blocks * regions)) // groups - 3


def row_coords():
    i = lax.broadcasted_iota(jnp.int32, (32, 128), 0)
    return i >> 3, (i >> 1) & 3, i & 1


def scatter_rows(out_ref, pieces):
    for half in range(2):
        total = jnp.zeros((32, 128), F32)
        for mask, row in pieces:
            total = total + jnp.where(mask, row[:, half * 128 : half * 128 + 128], 0.0)
        out_ref[:, half, :] = total


def gather_rows(ref, masks):
    halves = [ref[:, 0, :], ref[:, 1, :]]
    return [
        jnp.concatenate(
            [jnp.sum(jnp.where(m, h, 0.0), axis=0, keepdims=True) for h in halves], axis=1
        )
        for m in masks
    ]


def source_window(k, reg_ref, pat_ref, base, scale):
    rel = reg_ref[pl.ds(k, 1), :] - base
    w = lax.broadcasted_iota(jnp.int32, (WIN, B), 0)
    return jnp.where(w == rel, scale * pat_ref[pl.ds(k, 1), :], 0.0)


def composites_kernel(
    blocks, scale, low_hbm, up_hbm, pat_hbm, reg_hbm, par,
    own_ref, send_ref, low, up, pat, reg, src, xs, rs, sems, small
):
    run = blocks // PARTS
    last = blocks - 1

    def copies(k):
        return [
            pltpu.make_async_copy(low_hbm.at[k + i * run], low.at[k + i * run], sems.at[0, k + i * run])
            for i in range(PARTS)
        ] + [
            pltpu.make_async_copy(
                up_hbm.at[last - k - i * run], up.at[last - k - i * run], sems.at[1, last - k - i * run]
            )
            for i in range(PARTS)
        ]

    extras = (
        pltpu.make_async_copy(reg_hbm, reg, small.at[1]),
        pltpu.make_async_copy(pat_hbm, pat, small.at[2]),
    )

    def begin(k):
        if k < run:
            for c in copies(k):
                c.start()

    for c in extras:
        c.start()
    for k in range(DEPTH):
        begin(k)
    y, x, core = place()
    count = par.shape[0]
    base = window_base(blocks, count)
    for c in extras:
        c.wait()
    rel = reg[...] - base
    value = jnp.zeros((blocks, B), F32)
    for w in range(WIN):
        value = jnp.where(rel == w, par[jnp.clip(base + w, 0, count - 1)], value)
    src[...] = scale * pat[...] * value
    for k in range(run):
        for c in copies(k):
            c.wait()
        begin(k + DEPTH)
        if k == 0:
            for i in range(PARTS):
                xs[i, :B, :] = low[i * run].T
                xs[i, B:, :] = jnp.broadcast_to(src[i * run : i * run + 1, :], (AUG - B, B))
                rs[i] = up[last - i * run].T
            continue
        moved = [advance(xs[i], low[k + i * run]) for i in range(PARTS)]
        other = [advance(rs[i], up[last - k - i * run]) for i in range(PARTS)]
        for i in range(PARTS):
            row = k + i * run
            xs[i, :B, :] = moved[i][:B]
            xs[i, B:, :] = moved[i][B:] + src[row : row + 1, :]
            rs[i] = other[i]
    for i in (0, 2):
        moved = advance(xs[i], xs[i + 1, :B, :], NN)
        other = advance(rs[i], rs[i + 1], NN)
        xs[i, :B, :] = moved[:B]
        xs[i, B:, :] = moved[B:] + xs[i + 1, B:, :]
        rs[i] = other
    moved = advance(xs[0], xs[2, :B, :], NN)
    other = advance(rs[0], rs[2], NN)
    xs[1, :B, :] = moved[:B]
    xs[1, B:, :] = moved[B:] + xs[2, B:, :]
    rs[1] = other
    zero = jnp.zeros((AUG - B, B), F32)

    @pl.when(core == 0)
    def _():
        own_ref[...] = xs[1]
        send_ref[:B, :] = rs[1]
        send_ref[B:, :] = zero

    @pl.when(core != 0)
    def _():
        send_ref[...] = xs[1]
        own_ref[:B, :] = rs[1]
        own_ref[B:, :] = zero


def chip_kernel(own_ref, got_ref, out_ref):
    out_ref[...] = affine(own_ref[...], got_ref[...])


def prefixes_kernel(
    blocks, scale, low, piv_hbm, pat_ref, reg_ref, par_ref, cells_ref, values_ref, dep_ref,
    z_ref, f_ref, cnt_ref, sum_ref, pw_ref, piv, xa, xb, sems
):
    y, x, core = place()
    half = blocks // 2

    def copy(k):
        return pltpu.make_async_copy(piv_hbm.at[k], piv.at[k], sems.at[k])

    for k in range(blocks):
        copy(k).start()
    count = par_ref.shape[0]
    base = window_base(blocks, count)
    local = cells_ref[...] - ((y * 4 + x) * 2 + core) * (blocks * B)
    high = local >> 8
    low_part = local & 255
    which = jnp.where(lax.broadcasted_iota(jnp.int32, (blocks, B), 0) == high, 1.0, 0.0)
    slot = jnp.where(lax.broadcasted_iota(jnp.int32, (B, B), 0) == low_part, 1.0, 0.0).astype(BF16)
    weighted = which * values_ref[...]
    v1 = weighted.astype(BF16)
    v2, v3 = split(weighted - v1.astype(F32))
    d = functools.partial(lax.dot_general, dimension_numbers=NT, preferred_element_type=F32)
    cnt_ref[...] = d(which.astype(BF16), slot)
    sum_ref[...] = d(v1, slot) + (d(v2, slot) + d(v3, slot))
    wi = lax.broadcasted_iota(jnp.int32, (WIN, 128), 0)
    window = jnp.zeros((WIN, 128), F32)
    for w in range(WIN):
        window = jnp.where(wi == w, par_ref[jnp.clip(base + w, 0, count - 1)], window)
    pw_ref[...] = window

    def window(k):
        return source_window(k, reg_ref, pat_ref, base, scale)

    for ref, at in ((xa, 0), (xb, half)):
        ref[0, :B, :] = low[at].T
        ref[0, B:, :] = window(at)
    for k in range(1, half):
        a = advance(xa[k - 1], low[k])
        b = advance(xb[k - 1], low[k + half])
        xa[k, :B, :] = a[:B]
        xa[k, B:, :] = a[B:] + window(k)
        xb[k, :B, :] = b[:B]
        xb[k, B:, :] = b[B:] + window(k + half)
        if k == 2:
            for i in range(blocks):
                copy(i).wait()
        if k >= 2:
            z_ref[k - 2] = dot3(xa[k - 2], piv[k - 2], NT)
    for k in range(half):
        full = advance(xa[half - 1], xb[k, :B, :], NN)
        full = jnp.concatenate([full[:B], full[B:] + xb[k, B:, :]], axis=0)
        if k < 2:
            z_ref[half - 2 + k] = dot3(xa[half - 2 + k], piv[half - 2 + k], NT)
        z_ref[half + k] = dot3(full, piv[half + k], NT)
    f_ref[...] = full[B:]


def lines_kernel(blocks, up, z_ref, dep_ref, y_ref, token_ref, parts):
    half = blocks // 2
    last = blocks - 1
    y_ref[last, :ROWS, :] = z_ref[last]
    y_ref[last, ROWS:, :] = up[last].T
    parts[half - 1, :ROWS, :] = z_ref[half - 1]
    parts[half - 1, ROWS:, :] = up[half - 1].T
    for k in range(half - 2, -1, -1):
        a = advance(y_ref[k + half + 1], up[k + half])
        b = advance(parts[k + 1], up[k])
        y_ref[k + half, :ROWS, :] = a[:ROWS] + z_ref[k + half]
        y_ref[k + half, ROWS:, :] = a[ROWS:]
        parts[k, :ROWS, :] = b[:ROWS] + z_ref[k]
        parts[k, ROWS:, :] = b[ROWS:]
    for k in range(half):
        full = advance(y_ref[half], parts[k, ROWS:, :], NN)
        y_ref[k, :ROWS, :] = full[:ROWS] + parts[k, :ROWS, :]
        y_ref[k, ROWS:, :] = full[ROWS:]
    token_ref[...] = jnp.zeros((8, 128), F32)


def line_kernel(own_ref, mine_ref, r1_ref, r2_ref, r3_ref, dep_ref, maps_ref, row_ref, tail_ref):
    y, x, core = place()
    p = jnp.where(core == 0, x, 3 - x)
    i = lax.broadcasted_iota(jnp.int32, (AUG, B), 0)
    j = lax.broadcasted_iota(jnp.int32, (AUG, B), 1)
    eye = jnp.where(i == j, 1.0, 0.0)
    r1, r2, r3 = r1_ref[...], r2_ref[...], r3_ref[...]
    maps_ref[4] = mine_ref[...]
    maps_ref[0] = jnp.where(p >= 1, r1, eye)
    maps_ref[1] = jnp.where(p >= 2, r2, eye)
    pre = affine(jnp.where(p >= 3, r3, eye), maps_ref[1])
    suf = affine(jnp.where(p <= 2, r3, eye), jnp.where(p <= 1, r2, eye))
    maps_ref[2] = affine(pre, maps_ref[0])
    maps_ref[3] = affine(suf, jnp.where(p <= 0, r1, eye))
    row_ref[...] = affine(affine(maps_ref[2], own_ref[...]), maps_ref[3])
    tail_ref[...] = row_ref[B : B + 8, :]


def entering_kernel(own_ref, maps_ref, y1_ref, y2_ref, t3_ref, dep_ref, chip_ref, next_ref):
    y, x, core = place()
    t1 = jnp.where(y >= 1, y1_ref[B : B + 1, :], 0.0)
    t2 = jnp.where(y >= 2, y2_ref[B : B + 1, :], 0.0)
    t3 = jnp.where(y >= 3, t3_ref[0:1, :], 0.0)
    row = t1 + apply(t2 + apply(t3, y2_ref[:B, :]), y1_ref[:B, :])
    chip = maps_ref[2, B : B + 1, :] + apply(row, maps_ref[2, :B, :])
    following = own_ref[B : B + 1, :] + apply(chip, own_ref[:B, :])
    chip_ref[...] = jnp.broadcast_to(chip, (8, B))
    next_ref[...] = jnp.broadcast_to(following, (8, B))


def start_kernel(chip_ref, got_ref, pw_ref, y_ref, near1_ref, maps_ref, mapso_ref, dep1_ref, dep2_ref, in_ref, out_ref):
    my_y, my_x, core = place()
    entering = jnp.where(core == 0, chip_ref[0:1, :], got_ref[0:1, :])
    vb = jnp.concatenate([spread(entering), pw_ref[...]], axis=0)
    in_ref[...] = vb
    v = jnp.concatenate(
        [
            jnp.sum(vb * y_ref[0, :ROWS, :128], axis=0, keepdims=True),
            jnp.sum(vb * y_ref[0, :ROWS, 128:], axis=0, keepdims=True),
        ],
        axis=1,
    )
    z1 = jnp.where(core == 1, apply(v, near1_ref[:B, :]), v)
    z2 = apply(z1, jnp.where(core == 1, maps_ref[3, :B, :], mapso_ref[3, :B, :]))
    ty, tx, tc = row_coords()
    same = ty == my_y
    scatter_rows(
        out_ref,
        [
            (same & (tx == my_x) & (tc < core), v),
            (same & (tx < my_x), z1),
            (ty < my_y, z2),
        ],
    )


class Maps:
    def __init__(self, core, side, near, maps, steps):
        self.mine = core == side
        self.near_ref, self.map_refs, self.step_refs = near, maps, steps

    def near(self):
        return jnp.where(self.mine, self.near_ref[:B, :], self.map_refs[1][4, :B, :])

    def line(self, i):
        return jnp.where(self.mine, self.map_refs[0][i, :B, :], self.map_refs[1][i, :B, :])

    def step(self, j):
        mine, other = self.step_refs[j - 1]
        return jnp.where(self.mine, mine[:B, :], other[:B, :])


def spread_out(out_ref, first, m, leftward):
    my_y, my_x, core = place()
    side = 1 if leftward else 0
    g = jnp.where(core == side, apply_t(first, m.near()), first)
    g2 = apply_t(g, m.line(0))
    g3 = apply_t(g2, m.line(1))
    h = apply_t(g, m.line(2))
    h2 = apply_t(h, m.step(1))
    h3 = apply_t(h2, m.step(2))
    ty, tx, tc = row_coords()
    sign = -1 if leftward else 1
    dy, dx, dc = sign * (ty - my_y), sign * (tx - my_x), sign * (tc - core)
    same = dy == 0
    scatter_rows(
        out_ref,
        [
            (same & (dx == 0) & (dc > 0), first),
            (same & (dx == 1), g),
            (same & (dx == 2), g2),
            (same & (dx == 3), g3),
            (dy == 1, h),
            (dy == 2, h2),
            (dy == 3, h3),
        ],
    )


def collect(got_ref, m, leftward):
    my_y, my_x, core = place()
    sy, sx, sc = row_coords()
    same = sy == my_y
    part, mx, my = gather_rows(got_ref, [same & (sx == my_x), same & (sx != my_x), sy != my_y])
    total = mx + apply_t(my, m.line(3))
    side = 0 if leftward else 1
    return part + jnp.where(core == side, apply_t(total, m.near()), total)


def middle_kernel(
    blocks, got_ref, got0_ref, maps_ref, mapso_ref, y1_ref, y1o_ref, y2_ref, y2o_ref,
    in_ref, y_ref, cnt_ref, sum_ref, sol_ref, out_ref, acc_ref, sb, acc_r
):
    my_y, my_x, core = place()
    m = Maps(core, 1, got0_ref, (maps_ref, mapso_ref), ((y1_ref, y1o_ref), (y2_ref, y2o_ref)))
    sy, sx, sc = row_coords()
    same = sy == my_y
    part, t1, t2, t3, y1, y2, y3 = gather_rows(
        got_ref,
        [same & (sx == my_x)]
        + [same & (sx == my_x + j) for j in (1, 2, 3)]
        + [sy == my_y + j for j in (1, 2, 3)],
    )
    yv = y1 + apply(y2 + apply(y3, m.step(2)), m.step(1))
    xv = t1 + apply(t2 + apply(t3, m.line(1)), m.line(0)) + apply(yv, m.line(2))
    entering = part + jnp.where(core == 0, apply(xv, m.near()), xv)
    sb[...] = spread(entering)
    acc_ref[...] = jnp.zeros((ROWS, 128), F32)
    acc_r[...] = jnp.zeros((B, 128), F32)

    for k in range(blocks):
        vb, wb = in_ref[...], sb[...]
        row = jnp.concatenate(
            [
                jnp.sum(vb * y_ref[k, :ROWS, half], axis=0, keepdims=True)
                + jnp.sum(wb * y_ref[k, ROWS:, half], axis=0, keepdims=True)
                for half in (slice(0, 128), slice(128, 256))
            ],
            axis=1,
        )
        sol_ref[k : k + 1, :] = row
        forcing = cnt_ref[k : k + 1, :] * row - sum_ref[k : k + 1, :]
        left, right = forcing[:, :128], forcing[:, 128:]
        acc_ref[...] += y_ref[k, :ROWS, :128] * left + y_ref[k, :ROWS, 128:] * right
        acc_r[...] += y_ref[k, ROWS:, :128] * left + y_ref[k, ROWS:, 128:] * right

    acc_ref[...] = jnp.broadcast_to(jnp.sum(acc_ref[...], axis=1, keepdims=True), (ROWS, 128))
    first = to_row(jnp.sum(acc_r[...], axis=1, keepdims=True))
    spread_out(out_ref, first, m, False)


def return_kernel(
    got_ref, got0_ref, maps_ref, mapso_ref, y1_ref, y1o_ref, y2_ref, y2o_ref, acc_ref, y_ref,
    out_ref, gw_ref
):
    core = place()[2]
    upper = Maps(core, 1, got0_ref, (maps_ref, mapso_ref), None)
    lower = Maps(core, 0, got0_ref, (maps_ref, mapso_ref), ((y1_ref, y1o_ref), (y2_ref, y2o_ref)))
    c_in = collect(got_ref, upper, False)
    column = acc_ref[:, 0:1] + adjoint_column(c_in, y_ref[0, :ROWS, :])
    gw_ref[...] = jnp.broadcast_to(column[B:], (WIN, 128))
    spread_out(out_ref, to_row(column[:B]), lower, True)


def window_kernel(blocks, regions, got_ref, got0_ref, maps_ref, mapso_ref, gw_ref, f_ref, out_ref):
    core = place()[2]
    base = window_base(blocks, regions)
    lower = Maps(core, 0, got0_ref, (maps_ref, mapso_ref), None)
    a_in = collect(got_ref, lower, True)
    column = gw_ref[:, 0:1] + adjoint_column(a_in, f_ref[...])
    w = lax.broadcasted_iota(jnp.int32, (WIN, 128), 0)
    lane = lax.broadcasted_iota(jnp.int32, (WIN, 128), 1)
    row = jnp.sum(jnp.where(((base + w) & 127) == lane, column, 0.0), axis=0, keepdims=True)
    out_ref[...] = jnp.broadcast_to(row.reshape(1, 1, 128), out_ref.shape)


def total_kernel(blocks, groups, regions, tracers, got_ref, out_ref):
    total = got_ref[0:32, 0, :]
    for t in range(1, tracers):
        total = total + got_ref[32 * t : 32 * t + 32, 0, :]
    d = lax.broadcasted_iota(jnp.int32, (32, 128), 0)
    lane = lax.broadcasted_iota(jnp.int32, (32, 128), 1)
    base = (d * (blocks * regions)) // groups - 3
    tile = (base + ((lane - base) & 127)) >> 7
    for t in range(out_ref.shape[1] // 128 + 1):
        lo, hi = 128 * t, min(128 * t + 128, out_ref.shape[1])
        if hi > lo:
            row = jnp.sum(jnp.where(tile == t, total, 0.0), axis=0, keepdims=True)
            out_ref[:, lo:hi] = row[:, : hi - lo]


def device(y, x, core):
    return ((y % 4) * 4 + x % 4) * 2 + core


def shards(
    factor_lower, factor_pivot, factor_upper, source_pattern, regions, params, obs_cells, obs_values
):
    low, piv, up = factor_lower[0], factor_pivot[0], factor_upper[0]
    pat = source_pattern[0]
    blocks = low.shape[0]
    tracers = lax.axis_size("tracer")
    groups = blocks * lax.axis_size("sub")
    regions_all = params.shape[0]
    scale = float(groups) ** (-1.5)
    def shape(*dims):
        return jax.ShapeDtypeStruct(dims, F32)

    def near(*dims):
        return pltpu.VMEM(dims, F32)

    def far(*arrays):
        return [pltpu.with_memory_space_constraint(a, pltpu.HBM) for a in arrays]

    def call(kernel, outs, ins, scratch=(), limit=8, flops=0, traffic=0, name=None):
        return pl.pallas_call(
            kernel,
            out_shape=outs,
            in_specs=ins,
            out_specs=jax.tree.map(lambda _: VM, outs),
            scratch_shapes=list(scratch),
            compiler_params=pltpu.CompilerParams(vmem_limit_bytes=limit * MIB),
            cost_estimate=pl.CostEstimate(flops=flops, bytes_accessed=traffic, transcendentals=0),
            name=name,
        )

    def swap(a):
        return lax.ppermute(a, "sub", [(d, d ^ 1) for d in range(32)])

    def along_x(a, j):
        pairs = [(device(y, x, 0), device(y, x + j, 0)) for y in range(4) for x in range(4)]
        pairs += [(device(y, x, 1), device(y, x - j, 1)) for y in range(4) for x in range(4)]
        return lax.ppermute(a, "sub", pairs)

    def along_y(a, j):
        pairs = [(device(y, x, 0), device(y + j, x, 0)) for y in range(4) for x in range(4)]
        pairs += [(device(y, x, 1), device(y - j, x, 1)) for y in range(4) for x in range(4)]
        return lax.ppermute(a, "sub", pairs)

    def exchange(a):
        return lax.all_to_all(a, "sub", 0, 0)

    block = (blocks, B, B)
    own, send, low_near, up_near = call(
        functools.partial(composites_kernel, blocks, scale),
        (shape(AUG, B), shape(AUG, B), near(*block), near(*block)),
        [HBM] * 4 + [SM],
        [
            pltpu.VMEM((blocks, B), F32), pltpu.VMEM((blocks, B), jnp.int32),
            pltpu.VMEM((blocks, B), F32), pltpu.VMEM((PARTS, AUG, B), F32), pltpu.VMEM((PARTS, B, B), F32),
            pltpu.SemaphoreType.DMA((2, blocks)), pltpu.SemaphoreType.DMA((3,)),
        ],
        limit=12, flops=6 * 2 * 16 * B**3, traffic=8 * MIB, name="composites",
    )(*far(low, up, pat, regions), params)
    got = swap(send)
    chip = call(chip_kernel, shape(AUG, B), [VM, VM], flops=6 * B**3, name="chip")(own, got)
    r1, r2, r3 = [along_x(chip, j) for j in (1, 2, 3)]
    zt, ft, cnt, osum, pw = call(
        functools.partial(prefixes_kernel, blocks, scale),
        (near(blocks, ROWS, B), near(WIN, B), near(blocks, B), near(blocks, B), near(WIN, 128)),
        [VM, HBM, VM, VM, SM, VM, VM, ANY],
        [
            pltpu.VMEM(block, F32), pltpu.VMEM((blocks // 2, ROWS, B), F32),
            pltpu.VMEM((blocks // 2, ROWS, B), F32), pltpu.SemaphoreType.DMA((blocks,)),
        ],
        limit=14, flops=6 * 2 * 16 * B**3, traffic=8 * MIB, name="prefixes",
    )(low_near, *far(piv), pat, regions, params, obs_cells, obs_values, chip)
    maps, row, tail = call(
        line_kernel, (shape(5, AUG, B), shape(AUG, B), shape(8, B)), [VM, VM, VM, VM, VM, ANY],
        flops=6 * 6 * B**3, name="line",
    )(chip, own, r1, r2, r3, cnt)
    y1, y2, y3 = along_y(row, 1), along_y(row, 2), along_y(tail, 3)
    maps_o = swap(maps)
    yt, token = call(
        functools.partial(lines_kernel, blocks),
        (near(blocks, ROWS + B, B), near(8, 128)),
        [VM, VM, ANY],
        [pltpu.VMEM((blocks // 2, ROWS + B, B), F32)],
        limit=12, flops=6 * 3 * 16 * B**3, traffic=8 * MIB, name="lines",
    )(up_near, zt, y3)
    chip_in, following = call(
        entering_kernel, (shape(8, B), shape(8, B)), [VM] * 5 + [ANY], name="entering"
    )(own, maps, y1, y2, y3, token)
    following = swap(following)
    y1_o, y2_o = [swap(a) for a in lax.optimization_barrier((y1, y2, token))[:2]]
    messages = shape(32, 2, 128)
    vb, sent = call(start_kernel, (near(ROWS, 128), messages), [VM] * 7 + [ANY] * 2, name="start")(
        chip_in, following, pw, yt, got, maps, maps_o, y1_o, y2_o
    )
    got_s = exchange(sent)
    sol, sent, acc = call(
        functools.partial(middle_kernel, blocks),
        (shape(blocks, B), messages, near(ROWS, 128)),
        [VM] * 12,
        [pltpu.VMEM((B, 128), F32), pltpu.VMEM((B, 128), F32)],
        name="middle",
    )(got_s, got, maps, maps_o, y1, y1_o, y2, y2_o, vb, yt, cnt, osum)
    got_c = exchange(sent)
    sent, gw = call(return_kernel, (messages, near(WIN, 128)), [VM] * 10, name="return")(
        got_c, got, maps, maps_o, y1, y1_o, y2, y2_o, acc, yt
    )
    got_a = exchange(sent)
    sent = call(
        functools.partial(window_kernel, blocks, regions_all), shape(32 * tracers, 1, 128), [VM] * 6, name="window"
    )(got_a, got, maps, maps_o, gw, ft)
    spread_windows = lax.all_to_all(sent, ("tracer", "sub"), 0, 0)
    gradient = call(
        functools.partial(total_kernel, blocks, groups, regions_all, tracers), shape(1, regions_all), [VM],
        name="total",
    )(spread_windows)
    return (gradient.reshape(regions_all), sol[None])


def solution(mesh):
    return jax.shard_map(
        shards,
        mesh=mesh,
        in_specs=(
            P("tracer", "sub", None, None),
            P("tracer", "sub", None, None),
            P("tracer", "sub", None, None),
            P("tracer", "sub", None),
            P("sub", None),
            P(),
            P("tracer", "sub"),
            P("tracer", "sub"),
        ),
        out_specs=(P(), P("tracer", "sub", None)),
        check_vma=False,
    )
```

```python
import functools

import jax
import jax.numpy as jnp
from jax import lax
from jax.experimental import pallas as pl
from jax.experimental.pallas import tpu as pltpu
from jax.sharding import PartitionSpec as P

F32 = jnp.float32
BF16 = jnp.bfloat16
B = 256
AUG = 264
WIN = 32
ROWS = B + WIN
NT = (((1,), (1,)), ((), ()))
NN = (((1,), (0,)), ((), ()))
MIB = 1 << 20
PARTS = 4
DEPTH = 3
VM = pl.BlockSpec(memory_space=pltpu.VMEM)
SM = pl.BlockSpec(memory_space=pltpu.SMEM)
ANY = pl.BlockSpec(memory_space=pl.ANY)
HBM = pl.BlockSpec(memory_space=pltpu.HBM)


def split(a):
    high = a.astype(BF16)
    return high, (a - high.astype(F32)).astype(BF16)


def dot3(a, b, dims):
    ah, al = split(a)
    bh, bl = split(b)
    return lax.dot_general(
        jnp.concatenate([ah, ah, al], axis=1),
        jnp.concatenate([bh, bl, bh], axis=dims[0][1][0]),
        dims,
        preferred_element_type=F32,
    )


def less_unit(b):
    i = lax.broadcasted_iota(jnp.int32, (128, 128), 0)
    unit = jnp.where(i == lax.broadcasted_iota(jnp.int32, (128, 128), 1), 1.0, 0.0)
    top = jnp.concatenate([b[:128, :128] - unit, b[:128, 128:]], axis=1)
    return jnp.concatenate([top, jnp.concatenate([b[128:, :128], b[128:, 128:] - unit], axis=1)], axis=0)


def advance(a, b, dims=NT):
    return a + dot3(a, less_unit(b), dims)


def affine(first, second):
    product = advance(first, second[:B], NN)
    return jnp.concatenate([product[:B], product[B:] + second[B:]], axis=0)


def spread(row):
    return jnp.broadcast_to(row, (128, row.shape[1])).T


def apply(row, mt):
    vb = spread(row)
    return jnp.concatenate(
        [
            jnp.sum(vb * mt[:, :128], axis=0, keepdims=True),
            jnp.sum(vb * mt[:, 128:], axis=0, keepdims=True),
        ],
        axis=1,
    )


def adjoint_column(row, mt):
    acc = mt[:, :128] * row[:, :128] + mt[:, 128:] * row[:, 128:]
    return jnp.sum(acc, axis=1, keepdims=True)


def to_row(column):
    return jnp.broadcast_to(column, (column.shape[0], 128)).T[0:1]


def apply_t(row, mt):
    return to_row(adjoint_column(row, mt))


def place():
    sub = lax.axis_index("sub")
    return sub >> 3, (sub >> 1) & 3, sub & 1


def window_base(blocks, regions):
    groups = blocks * lax.axis_size("sub")
    return (lax.axis_index("sub") * (blocks * regions)) // groups - 3


def row_coords():
    i = lax.broadcasted_iota(jnp.int32, (32, 128), 0)
    return i >> 3, (i >> 1) & 3, i & 1


def scatter_rows(out_ref, pieces):
    for half in range(2):
        total = jnp.zeros((32, 128), F32)
        for mask, row in pieces:
            total = total + jnp.where(mask, row[:, half * 128 : half * 128 + 128], 0.0)
        out_ref[:, half, :] = total


def gather_rows(ref, masks):
    halves = [ref[:, 0, :], ref[:, 1, :]]
    return [
        jnp.concatenate(
            [jnp.sum(jnp.where(m, h, 0.0), axis=0, keepdims=True) for h in halves], axis=1
        )
        for m in masks
    ]


def source_window(k, reg_ref, pat_ref, base, scale):
    rel = reg_ref[pl.ds(k, 1), :] - base
    w = lax.broadcasted_iota(jnp.int32, (WIN, B), 0)
    return jnp.where(w == rel, scale * pat_ref[pl.ds(k, 1), :], 0.0)


def composites_kernel(
    blocks, scale, low_hbm, up_hbm, pat_hbm, reg_hbm, par,
    own_ref, send_ref, low, up, pat, reg, src, xs, rs, sems, small
):
    run = blocks // PARTS
    last = blocks - 1

    def copies(k):
        return [
            pltpu.make_async_copy(low_hbm.at[k + i * run], low.at[k + i * run], sems.at[0, k + i * run])
            for i in range(PARTS)
        ] + [
            pltpu.make_async_copy(
                up_hbm.at[last - k - i * run], up.at[last - k - i * run], sems.at[1, last - k - i * run]
            )
            for i in range(PARTS)
        ]

    extras = (
        pltpu.make_async_copy(reg_hbm, reg, small.at[1]),
        pltpu.make_async_copy(pat_hbm, pat, small.at[2]),
    )

    def begin(k):
        if k < run:
            for c in copies(k):
                c.start()

    for c in extras:
        c.start()
    for k in range(DEPTH):
        begin(k)
    y, x, core = place()
    count = par.shape[0]
    base = window_base(blocks, count)
    for c in extras:
        c.wait()
    rel = reg[...] - base
    value = jnp.zeros((blocks, B), F32)
    for w in range(WIN):
        value = jnp.where(rel == w, par[jnp.clip(base + w, 0, count - 1)], value)
    src[...] = scale * pat[...] * value
    for k in range(run):
        for c in copies(k):
            c.wait()
        begin(k + DEPTH)
        if k == 0:
            for i in range(PARTS):
                xs[i, :B, :] = low[i * run].T
                xs[i, B:, :] = jnp.broadcast_to(src[i * run : i * run + 1, :], (AUG - B, B))
                rs[i] = up[last - i * run].T
            continue
        moved = [advance(xs[i], low[k + i * run]) for i in range(PARTS)]
        other = [advance(rs[i], up[last - k - i * run]) for i in range(PARTS)]
        for i in range(PARTS):
            row = k + i * run
            xs[i, :B, :] = moved[i][:B]
            xs[i, B:, :] = moved[i][B:] + src[row : row + 1, :]
            rs[i] = other[i]
    for i in (0, 2):
        moved = advance(xs[i], xs[i + 1, :B, :], NN)
        other = advance(rs[i], rs[i + 1], NN)
        xs[i, :B, :] = moved[:B]
        xs[i, B:, :] = moved[B:] + xs[i + 1, B:, :]
        rs[i] = other
    moved = advance(xs[0], xs[2, :B, :], NN)
    other = advance(rs[0], rs[2], NN)
    xs[1, :B, :] = moved[:B]
    xs[1, B:, :] = moved[B:] + xs[2, B:, :]
    rs[1] = other
    zero = jnp.zeros((AUG - B, B), F32)

    @pl.when(core == 0)
    def _():
        own_ref[...] = xs[1]
        send_ref[:B, :] = rs[1]
        send_ref[B:, :] = zero

    @pl.when(core != 0)
    def _():
        send_ref[...] = xs[1]
        own_ref[:B, :] = rs[1]
        own_ref[B:, :] = zero


def chip_kernel(own_ref, got_ref, out_ref):
    out_ref[...] = affine(own_ref[...], got_ref[...])


def prefixes_kernel(
    blocks, scale, low, piv_hbm, pat_ref, reg_ref, par_ref, cells_ref, values_ref, dep_ref,
    z_ref, f_ref, cnt_ref, sum_ref, pw_ref, piv, xa, xb, sems
):
    y, x, core = place()
    half = blocks // 2

    def copy(k):
        return pltpu.make_async_copy(piv_hbm.at[k], piv.at[k], sems.at[k])

    for k in range(blocks):
        copy(k).start()
    count = par_ref.shape[0]
    base = window_base(blocks, count)
    local = cells_ref[...] - ((y * 4 + x) * 2 + core) * (blocks * B)
    high = local >> 8
    low_part = local & 255
    which = jnp.where(lax.broadcasted_iota(jnp.int32, (blocks, B), 0) == high, 1.0, 0.0)
    slot = jnp.where(lax.broadcasted_iota(jnp.int32, (B, B), 0) == low_part, 1.0, 0.0).astype(BF16)
    weighted = which * values_ref[...]
    v1 = weighted.astype(BF16)
    v2, v3 = split(weighted - v1.astype(F32))
    d = functools.partial(lax.dot_general, dimension_numbers=NT, preferred_element_type=F32)
    cnt_ref[...] = d(which.astype(BF16), slot)
    sum_ref[...] = d(v1, slot) + (d(v2, slot) + d(v3, slot))
    wi = lax.broadcasted_iota(jnp.int32, (WIN, 128), 0)
    window = jnp.zeros((WIN, 128), F32)
    for w in range(WIN):
        window = jnp.where(wi == w, par_ref[jnp.clip(base + w, 0, count - 1)], window)
    pw_ref[...] = window

    def window(k):
        return source_window(k, reg_ref, pat_ref, base, scale)

    for ref, at in ((xa, 0), (xb, half)):
        ref[0, :B, :] = low[at].T
        ref[0, B:, :] = window(at)
    for k in range(1, half):
        a = advance(xa[k - 1], low[k])
        b = advance(xb[k - 1], low[k + half])
        xa[k, :B, :] = a[:B]
        xa[k, B:, :] = a[B:] + window(k)
        xb[k, :B, :] = b[:B]
        xb[k, B:, :] = b[B:] + window(k + half)
        if k == 2:
            for i in range(blocks):
                copy(i).wait()
        if k >= 2:
            z_ref[k - 2] = dot3(xa[k - 2], piv[k - 2], NT)
    for k in range(half):
        full = advance(xa[half - 1], xb[k, :B, :], NN)
        full = jnp.concatenate([full[:B], full[B:] + xb[k, B:, :]], axis=0)
        if k < 2:
            z_ref[half - 2 + k] = dot3(xa[half - 2 + k], piv[half - 2 + k], NT)
        z_ref[half + k] = dot3(full, piv[half + k], NT)
    f_ref[...] = full[B:]


def lines_kernel(blocks, up, z_ref, dep_ref, y_ref, token_ref, parts):
    half = blocks // 2
    last = blocks - 1
    y_ref[last, :ROWS, :] = z_ref[last]
    y_ref[last, ROWS:, :] = up[last].T
    parts[half - 1, :ROWS, :] = z_ref[half - 1]
    parts[half - 1, ROWS:, :] = up[half - 1].T
    for k in range(half - 2, -1, -1):
        a = advance(y_ref[k + half + 1], up[k + half])
        b = advance(parts[k + 1], up[k])
        y_ref[k + half, :ROWS, :] = a[:ROWS] + z_ref[k + half]
        y_ref[k + half, ROWS:, :] = a[ROWS:]
        parts[k, :ROWS, :] = b[:ROWS] + z_ref[k]
        parts[k, ROWS:, :] = b[ROWS:]
    for k in range(half):
        full = advance(y_ref[half], parts[k, ROWS:, :], NN)
        y_ref[k, :ROWS, :] = full[:ROWS] + parts[k, :ROWS, :]
        y_ref[k, ROWS:, :] = full[ROWS:]
    token_ref[...] = jnp.zeros((8, 128), F32)


def line_kernel(own_ref, mine_ref, r1_ref, r2_ref, r3_ref, dep_ref, maps_ref, row_ref, tail_ref):
    y, x, core = place()
    p = jnp.where(core == 0, x, 3 - x)
    i = lax.broadcasted_iota(jnp.int32, (AUG, B), 0)
    j = lax.broadcasted_iota(jnp.int32, (AUG, B), 1)
    eye = jnp.where(i == j, 1.0, 0.0)
    r1, r2, r3 = r1_ref[...], r2_ref[...], r3_ref[...]
    maps_ref[4] = mine_ref[...]
    maps_ref[0] = jnp.where(p >= 1, r1, eye)
    maps_ref[1] = jnp.where(p >= 2, r2, eye)
    pre = affine(jnp.where(p >= 3, r3, eye), maps_ref[1])
    suf = affine(jnp.where(p <= 2, r3, eye), jnp.where(p <= 1, r2, eye))
    maps_ref[2] = affine(pre, maps_ref[0])
    maps_ref[3] = affine(suf, jnp.where(p <= 0, r1, eye))
    row_ref[...] = affine(affine(maps_ref[2], own_ref[...]), maps_ref[3])
    tail_ref[...] = row_ref[B : B + 8, :]


def entering_kernel(own_ref, maps_ref, y1_ref, y2_ref, t3_ref, dep_ref, chip_ref, next_ref):
    y, x, core = place()
    t1 = jnp.where(y >= 1, y1_ref[B : B + 1, :], 0.0)
    t2 = jnp.where(y >= 2, y2_ref[B : B + 1, :], 0.0)
    t3 = jnp.where(y >= 3, t3_ref[0:1, :], 0.0)
    row = t1 + apply(t2 + apply(t3, y2_ref[:B, :]), y1_ref[:B, :])
    chip = maps_ref[2, B : B + 1, :] + apply(row, maps_ref[2, :B, :])
    following = own_ref[B : B + 1, :] + apply(chip, own_ref[:B, :])
    chip_ref[...] = jnp.broadcast_to(chip, (8, B))
    next_ref[...] = jnp.broadcast_to(following, (8, B))


def start_kernel(chip_ref, got_ref, pw_ref, y_ref, near1_ref, maps_ref, mapso_ref, dep1_ref, dep2_ref, in_ref, out_ref):
    my_y, my_x, core = place()
    entering = jnp.where(core == 0, chip_ref[0:1, :], got_ref[0:1, :])
    vb = jnp.concatenate([spread(entering), pw_ref[...]], axis=0)
    in_ref[...] = vb
    v = jnp.concatenate(
        [
            jnp.sum(vb * y_ref[0, :ROWS, :128], axis=0, keepdims=True),
            jnp.sum(vb * y_ref[0, :ROWS, 128:], axis=0, keepdims=True),
        ],
        axis=1,
    )
    z1 = jnp.where(core == 1, apply(v, near1_ref[:B, :]), v)
    z2 = apply(z1, jnp.where(core == 1, maps_ref[3, :B, :], mapso_ref[3, :B, :]))
    ty, tx, tc = row_coords()
    same = ty == my_y
    scatter_rows(
        out_ref,
        [
            (same & (tx == my_x) & (tc < core), v),
            (same & (tx < my_x), z1),
            (ty < my_y, z2),
        ],
    )


class Maps:
    def __init__(self, core, side, near, maps, steps):
        self.mine = core == side
        self.near_ref, self.map_refs, self.step_refs = near, maps, steps

    def near(self):
        return jnp.where(self.mine, self.near_ref[:B, :], self.map_refs[1][4, :B, :])

    def line(self, i):
        return jnp.where(self.mine, self.map_refs[0][i, :B, :], self.map_refs[1][i, :B, :])

    def step(self, j):
        mine, other = self.step_refs[j - 1]
        return jnp.where(self.mine, mine[:B, :], other[:B, :])


def spread_out(out_ref, first, m, leftward):
    my_y, my_x, core = place()
    side = 1 if leftward else 0
    g = jnp.where(core == side, apply_t(first, m.near()), first)
    g2 = apply_t(g, m.line(0))
    g3 = apply_t(g2, m.line(1))
    h = apply_t(g, m.line(2))
    h2 = apply_t(h, m.step(1))
    h3 = apply_t(h2, m.step(2))
    ty, tx, tc = row_coords()
    sign = -1 if leftward else 1
    dy, dx, dc = sign * (ty - my_y), sign * (tx - my_x), sign * (tc - core)
    same = dy == 0
    scatter_rows(
        out_ref,
        [
            (same & (dx == 0) & (dc > 0), first),
            (same & (dx == 1), g),
            (same & (dx == 2), g2),
            (same & (dx == 3), g3),
            (dy == 1, h),
            (dy == 2, h2),
            (dy == 3, h3),
        ],
    )


def collect(got_ref, m, leftward):
    my_y, my_x, core = place()
    sy, sx, sc = row_coords()
    same = sy == my_y
    part, mx, my = gather_rows(got_ref, [same & (sx == my_x), same & (sx != my_x), sy != my_y])
    total = mx + apply_t(my, m.line(3))
    side = 0 if leftward else 1
    return part + jnp.where(core == side, apply_t(total, m.near()), total)


def middle_kernel(
    blocks, got_ref, got0_ref, maps_ref, mapso_ref, y1_ref, y1o_ref, y2_ref, y2o_ref,
    in_ref, y_ref, cnt_ref, sum_ref, sol_ref, out_ref, acc_ref, sb, acc_r
):
    my_y, my_x, core = place()
    m = Maps(core, 1, got0_ref, (maps_ref, mapso_ref), ((y1_ref, y1o_ref), (y2_ref, y2o_ref)))
    sy, sx, sc = row_coords()
    same = sy == my_y
    part, t1, t2, t3, y1, y2, y3 = gather_rows(
        got_ref,
        [same & (sx == my_x)]
        + [same & (sx == my_x + j) for j in (1, 2, 3)]
        + [sy == my_y + j for j in (1, 2, 3)],
    )
    yv = y1 + apply(y2 + apply(y3, m.step(2)), m.step(1))
    xv = t1 + apply(t2 + apply(t3, m.line(1)), m.line(0)) + apply(yv, m.line(2))
    entering = part + jnp.where(core == 0, apply(xv, m.near()), xv)
    sb[...] = spread(entering)
    acc_ref[...] = jnp.zeros((ROWS, 128), F32)
    acc_r[...] = jnp.zeros((B, 128), F32)

    for k in range(blocks):
        vb, wb = in_ref[...], sb[...]
        row = jnp.concatenate(
            [
                jnp.sum(vb * y_ref[k, :ROWS, half], axis=0, keepdims=True)
                + jnp.sum(wb * y_ref[k, ROWS:, half], axis=0, keepdims=True)
                for half in (slice(0, 128), slice(128, 256))
            ],
            axis=1,
        )
        sol_ref[k : k + 1, :] = row
        forcing = cnt_ref[k : k + 1, :] * row - sum_ref[k : k + 1, :]
        left, right = forcing[:, :128], forcing[:, 128:]
        acc_ref[...] += y_ref[k, :ROWS, :128] * left + y_ref[k, :ROWS, 128:] * right
        acc_r[...] += y_ref[k, ROWS:, :128] * left + y_ref[k, ROWS:, 128:] * right

    acc_ref[...] = jnp.broadcast_to(jnp.sum(acc_ref[...], axis=1, keepdims=True), (ROWS, 128))
    first = to_row(jnp.sum(acc_r[...], axis=1, keepdims=True))
    spread_out(out_ref, first, m, False)


def return_kernel(
    got_ref, got0_ref, maps_ref, mapso_ref, y1_ref, y1o_ref, y2_ref, y2o_ref, acc_ref, y_ref,
    out_ref, gw_ref
):
    core = place()[2]
    upper = Maps(core, 1, got0_ref, (maps_ref, mapso_ref), None)
    lower = Maps(core, 0, got0_ref, (maps_ref, mapso_ref), ((y1_ref, y1o_ref), (y2_ref, y2o_ref)))
    c_in = collect(got_ref, upper, False)
    column = acc_ref[:, 0:1] + adjoint_column(c_in, y_ref[0, :ROWS, :])
    gw_ref[...] = jnp.broadcast_to(column[B:], (WIN, 128))
    spread_out(out_ref, to_row(column[:B]), lower, True)


def window_kernel(blocks, regions, got_ref, got0_ref, maps_ref, mapso_ref, gw_ref, f_ref, out_ref):
    core = place()[2]
    base = window_base(blocks, regions)
    lower = Maps(core, 0, got0_ref, (maps_ref, mapso_ref), None)
    a_in = collect(got_ref, lower, True)
    column = gw_ref[:, 0:1] + adjoint_column(a_in, f_ref[...])
    w = lax.broadcasted_iota(jnp.int32, (WIN, 128), 0)
    lane = lax.broadcasted_iota(jnp.int32, (WIN, 128), 1)
    row = jnp.sum(jnp.where(((base + w) & 127) == lane, column, 0.0), axis=0, keepdims=True)
    out_ref[...] = jnp.broadcast_to(row.reshape(1, 1, 128), out_ref.shape)


def total_kernel(blocks, groups, regions, tracers, got_ref, out_ref):
    total = got_ref[0:32, 0, :]
    for t in range(1, tracers):
        total = total + got_ref[32 * t : 32 * t + 32, 0, :]
    d = lax.broadcasted_iota(jnp.int32, (32, 128), 0)
    lane = lax.broadcasted_iota(jnp.int32, (32, 128), 1)
    base = (d * (blocks * regions)) // groups - 3
    tile = (base + ((lane - base) & 127)) >> 7
    for t in range(out_ref.shape[1] // 128 + 1):
        lo, hi = 128 * t, min(128 * t + 128, out_ref.shape[1])
        if hi > lo:
            row = jnp.sum(jnp.where(tile == t, total, 0.0), axis=0, keepdims=True)
            out_ref[:, lo:hi] = row[:, : hi - lo]


def device(y, x, core):
    return ((y % 4) * 4 + x % 4) * 2 + core


def shards(
    factor_lower, factor_pivot, factor_upper, source_pattern, regions, params, obs_cells, obs_values
):
    low, piv, up = factor_lower[0], factor_pivot[0], factor_upper[0]
    pat = source_pattern[0]
    blocks = low.shape[0]
    tracers = lax.axis_size("tracer")
    groups = blocks * lax.axis_size("sub")
    regions_all = params.shape[0]
    scale = float(groups) ** (-1.5)
    def shape(*dims):
        return jax.ShapeDtypeStruct(dims, F32)

    def near(*dims):
        return pltpu.VMEM(dims, F32)

    def far(*arrays):
        return [pltpu.with_memory_space_constraint(a, pltpu.HBM) for a in arrays]

    def call(kernel, outs, ins, scratch=(), limit=8, flops=0, traffic=0, name=None):
        return pl.pallas_call(
            kernel,
            out_shape=outs,
            in_specs=ins,
            out_specs=jax.tree.map(lambda _: VM, outs),
            scratch_shapes=list(scratch),
            compiler_params=pltpu.CompilerParams(vmem_limit_bytes=limit * MIB),
            cost_estimate=pl.CostEstimate(flops=flops, bytes_accessed=traffic, transcendentals=0),
            name=name,
        )

    def swap(a):
        return lax.ppermute(a, "sub", [(d, d ^ 1) for d in range(32)])

    def along_x(a, j):
        pairs = [(device(y, x, 0), device(y, x + j, 0)) for y in range(4) for x in range(4)]
        pairs += [(device(y, x, 1), device(y, x - j, 1)) for y in range(4) for x in range(4)]
        return lax.ppermute(a, "sub", pairs)

    def along_y(a, j):
        pairs = [(device(y, x, 0), device(y + j, x, 0)) for y in range(4) for x in range(4)]
        pairs += [(device(y, x, 1), device(y - j, x, 1)) for y in range(4) for x in range(4)]
        return lax.ppermute(a, "sub", pairs)

    def exchange(a):
        return lax.all_to_all(a, "sub", 0, 0)

    block = (blocks, B, B)
    own, send, low_near, up_near = call(
        functools.partial(composites_kernel, blocks, scale),
        (shape(AUG, B), shape(AUG, B), near(*block), near(*block)),
        [HBM] * 4 + [SM],
        [
            pltpu.VMEM((blocks, B), F32), pltpu.VMEM((blocks, B), jnp.int32),
            pltpu.VMEM((blocks, B), F32), pltpu.VMEM((PARTS, AUG, B), F32), pltpu.VMEM((PARTS, B, B), F32),
            pltpu.SemaphoreType.DMA((2, blocks)), pltpu.SemaphoreType.DMA((3,)),
        ],
        limit=12, flops=6 * 2 * 16 * B**3, traffic=8 * MIB, name="composites",
    )(*far(low, up, pat, regions), params)
    got = swap(send)
    chip = call(chip_kernel, shape(AUG, B), [VM, VM], flops=6 * B**3, name="chip")(own, got)
    r1, r2, r3 = [along_x(chip, j) for j in (1, 2, 3)]
    zt, ft, cnt, osum, pw = call(
        functools.partial(prefixes_kernel, blocks, scale),
        (near(blocks, ROWS, B), near(WIN, B), near(blocks, B), near(blocks, B), near(WIN, 128)),
        [VM, HBM, VM, VM, SM, VM, VM, ANY],
        [
            pltpu.VMEM(block, F32), pltpu.VMEM((blocks // 2, ROWS, B), F32),
            pltpu.VMEM((blocks // 2, ROWS, B), F32), pltpu.SemaphoreType.DMA((blocks,)),
        ],
        limit=14, flops=6 * 2 * 16 * B**3, traffic=8 * MIB, name="prefixes",
    )(low_near, *far(piv), pat, regions, params, obs_cells, obs_values, chip)
    maps, row, tail = call(
        line_kernel, (shape(5, AUG, B), shape(AUG, B), shape(8, B)), [VM, VM, VM, VM, VM, ANY],
        flops=6 * 6 * B**3, name="line",
    )(chip, own, r1, r2, r3, cnt)
    y1, y2, y3 = along_y(row, 1), along_y(row, 2), along_y(tail, 3)
    maps_o = swap(maps)
    yt, token = call(
        functools.partial(lines_kernel, blocks),
        (near(blocks, ROWS + B, B), near(8, 128)),
        [VM, VM, ANY],
        [pltpu.VMEM((blocks // 2, ROWS + B, B), F32)],
        limit=12, flops=6 * 3 * 16 * B**3, traffic=8 * MIB, name="lines",
    )(up_near, zt, y3)
    chip_in, following = call(
        entering_kernel, (shape(8, B), shape(8, B)), [VM] * 5 + [ANY], name="entering"
    )(own, maps, y1, y2, y3, token)
    following = swap(following)
    y1_o, y2_o = [swap(a) for a in lax.optimization_barrier((y1, y2, token))[:2]]
    messages = shape(32, 2, 128)
    vb, sent = call(start_kernel, (near(ROWS, 128), messages), [VM] * 7 + [ANY] * 2, name="start")(
        chip_in, following, pw, yt, got, maps, maps_o, y1_o, y2_o
    )
    got_s = exchange(sent)
    sol, sent, acc = call(
        functools.partial(middle_kernel, blocks),
        (shape(blocks, B), messages, near(ROWS, 128)),
        [VM] * 12,
        [pltpu.VMEM((B, 128), F32), pltpu.VMEM((B, 128), F32)],
        name="middle",
    )(got_s, got, maps, maps_o, y1, y1_o, y2, y2_o, vb, yt, cnt, osum)
    got_c = exchange(sent)
    sent, gw = call(return_kernel, (messages, near(WIN, 128)), [VM] * 10, name="return")(
        got_c, got, maps, maps_o, y1, y1_o, y2, y2_o, acc, yt
    )
    got_a = exchange(sent)
    sent = call(
        functools.partial(window_kernel, blocks, regions_all), shape(32 * tracers, 1, 128), [VM] * 6, name="window"
    )(got_a, got, maps, maps_o, gw, ft)
    spread_windows = lax.all_to_all(sent, ("tracer", "sub"), 0, 0)
    gradient = call(
        functools.partial(total_kernel, blocks, groups, regions_all, tracers), shape(1, regions_all), [VM],
        name="total",
    )(spread_windows)
    return (gradient.reshape(regions_all), sol[None])


def solution(mesh):
    return jax.shard_map(
        shards,
        mesh=mesh,
        in_specs=(
            P("tracer", "sub", None, None),
            P("tracer", "sub", None, None),
            P("tracer", "sub", None, None),
            P("tracer", "sub", None),
            P("sub", None),
            P(),
            P("tracer", "sub"),
            P("tracer", "sub"),
        ),
        out_specs=(P(), P("tracer", "sub", None)),
        check_vma=False,
    )
```

```python
import functools

import jax
import jax.numpy as jnp
from jax import lax
from jax.experimental import pallas as pl
from jax.experimental.pallas import tpu as pltpu
from jax.sharding import PartitionSpec as P

F32 = jnp.float32
BF16 = jnp.bfloat16
B = 256
AUG = 264
WIN = 32
ROWS = B + WIN
NT = (((1,), (1,)), ((), ()))
NN = (((1,), (0,)), ((), ()))
MIB = 1 << 20
PARTS = 4
DEPTH = 2
VM = pl.BlockSpec(memory_space=pltpu.VMEM)
SM = pl.BlockSpec(memory_space=pltpu.SMEM)
ANY = pl.BlockSpec(memory_space=pl.ANY)
HBM = pl.BlockSpec(memory_space=pltpu.HBM)


def split(a):
    high = a.astype(BF16)
    return high, (a - high.astype(F32)).astype(BF16)


def dot3(a, b, dims):
    ah, al = split(a)
    bh, bl = split(b)
    return lax.dot_general(
        jnp.concatenate([ah, ah, al], axis=1),
        jnp.concatenate([bh, bl, bh], axis=dims[0][1][0]),
        dims,
        preferred_element_type=F32,
    )


def less_unit(b):
    i = lax.broadcasted_iota(jnp.int32, (128, 128), 0)
    unit = jnp.where(i == lax.broadcasted_iota(jnp.int32, (128, 128), 1), 1.0, 0.0)
    top = jnp.concatenate([b[:128, :128] - unit, b[:128, 128:]], axis=1)
    return jnp.concatenate([top, jnp.concatenate([b[128:, :128], b[128:, 128:] - unit], axis=1)], axis=0)


def advance(a, b, dims=NT):
    return a + dot3(a, less_unit(b), dims)


def affine(first, second):
    product = advance(first, second[:B], NN)
    return jnp.concatenate([product[:B], product[B:] + second[B:]], axis=0)


def spread(row):
    return jnp.broadcast_to(row, (128, row.shape[1])).T


def apply(row, mt):
    vb = spread(row)
    return jnp.concatenate(
        [
            jnp.sum(vb * mt[:, :128], axis=0, keepdims=True),
            jnp.sum(vb * mt[:, 128:], axis=0, keepdims=True),
        ],
        axis=1,
    )


def adjoint_column(row, mt):
    acc = mt[:, :128] * row[:, :128] + mt[:, 128:] * row[:, 128:]
    return jnp.sum(acc, axis=1, keepdims=True)


def to_row(column):
    return jnp.broadcast_to(column, (column.shape[0], 128)).T[0:1]


def apply_t(row, mt):
    return to_row(adjoint_column(row, mt))


def place():
    sub = lax.axis_index("sub")
    return sub >> 3, (sub >> 1) & 3, sub & 1


def window_base(blocks, regions):
    groups = blocks * lax.axis_size("sub")
    return (lax.axis_index("sub") * (blocks * regions)) // groups - 3


def row_coords():
    i = lax.broadcasted_iota(jnp.int32, (32, 128), 0)
    return i >> 3, (i >> 1) & 3, i & 1


def scatter_rows(out_ref, pieces):
    for half in range(2):
        total = jnp.zeros((32, 128), F32)
        for mask, row in pieces:
            total = total + jnp.where(mask, row[:, half * 128 : half * 128 + 128], 0.0)
        out_ref[:, half, :] = total


def gather_rows(ref, masks):
    halves = [ref[:, 0, :], ref[:, 1, :]]
    return [
        jnp.concatenate(
            [jnp.sum(jnp.where(m, h, 0.0), axis=0, keepdims=True) for h in halves], axis=1
        )
        for m in masks
    ]


def source_window(k, reg_ref, pat_ref, base, scale):
    rel = reg_ref[pl.ds(k, 1), :] - base
    w = lax.broadcasted_iota(jnp.int32, (WIN, B), 0)
    return jnp.where(w == rel, scale * pat_ref[pl.ds(k, 1), :], 0.0)


def composites_kernel(
    blocks, scale, low_hbm, up_hbm, pat_hbm, reg_hbm, par,
    own_ref, send_ref, low, up, pat, reg, src, xs, rs, sems, small
):
    run = blocks // PARTS
    last = blocks - 1

    def copies(k):
        return [
            pltpu.make_async_copy(low_hbm.at[k + i * run], low.at[k + i * run], sems.at[0, k + i * run])
            for i in range(PARTS)
        ] + [
            pltpu.make_async_copy(
                up_hbm.at[last - k - i * run], up.at[last - k - i * run], sems.at[1, last - k - i * run]
            )
            for i in range(PARTS)
        ]

    extras = (
        pltpu.make_async_copy(reg_hbm, reg, small.at[1]),
        pltpu.make_async_copy(pat_hbm, pat, small.at[2]),
    )

    def begin(k):
        if k < run:
            for c in copies(k):
                c.start()

    for c in extras:
        c.start()
    begin(0)
    y, x, core = place()
    count = par.shape[0]
    base = window_base(blocks, count)
    for c in extras:
        c.wait()
    rel = reg[...] - base
    value = jnp.zeros((blocks, B), F32)
    for w in range(WIN):
        value = jnp.where(rel == w, par[jnp.clip(base + w, 0, count - 1)], value)
    src[...] = scale * pat[...] * value
    for k in range(1, DEPTH):
        begin(k)
    for k in range(run):
        for c in copies(k):
            c.wait()
        begin(k + DEPTH)
        if k == 0:
            for i in range(PARTS):
                xs[i, :B, :] = low[i * run].T
                xs[i, B:, :] = jnp.broadcast_to(src[i * run : i * run + 1, :], (AUG - B, B))
                rs[i] = up[last - i * run].T
            continue
        moved = [advance(xs[i], low[k + i * run]) for i in range(PARTS)]
        other = [advance(rs[i], up[last - k - i * run]) for i in range(PARTS)]
        for i in range(PARTS):
            row = k + i * run
            xs[i, :B, :] = moved[i][:B]
            xs[i, B:, :] = moved[i][B:] + src[row : row + 1, :]
            rs[i] = other[i]
    for i in (0, 2):
        moved = advance(xs[i], xs[i + 1, :B, :], NN)
        other = advance(rs[i], rs[i + 1], NN)
        xs[i, :B, :] = moved[:B]
        xs[i, B:, :] = moved[B:] + xs[i + 1, B:, :]
        rs[i] = other
    moved = advance(xs[0], xs[2, :B, :], NN)
    other = advance(rs[0], rs[2], NN)
    xs[1, :B, :] = moved[:B]
    xs[1, B:, :] = moved[B:] + xs[2, B:, :]
    rs[1] = other
    zero = jnp.zeros((AUG - B, B), F32)

    @pl.when(core == 0)
    def _():
        own_ref[...] = xs[1]
        send_ref[:B, :] = rs[1]
        send_ref[B:, :] = zero

    @pl.when(core != 0)
    def _():
        send_ref[...] = xs[1]
        own_ref[:B, :] = rs[1]
        own_ref[B:, :] = zero


def chip_kernel(own_ref, got_ref, out_ref):
    out_ref[...] = affine(own_ref[...], got_ref[...])


def prefixes_kernel(
    blocks, scale, low, piv_hbm, pat_ref, reg_ref, par_ref, cells_ref, values_ref, dep_ref,
    z_ref, f_ref, cnt_ref, sum_ref, pw_ref, piv, xa, xb, sems
):
    y, x, core = place()
    half = blocks // 2

    def copy(k):
        return pltpu.make_async_copy(piv_hbm.at[k], piv.at[k], sems.at[k])

    for k in range(blocks):
        copy(k).start()
    count = par_ref.shape[0]
    base = window_base(blocks, count)
    local = cells_ref[...] - ((y * 4 + x) * 2 + core) * (blocks * B)
    high = local >> 8
    low_part = local & 255
    which = jnp.where(lax.broadcasted_iota(jnp.int32, (blocks, B), 0) == high, 1.0, 0.0)
    slot = jnp.where(lax.broadcasted_iota(jnp.int32, (B, B), 0) == low_part, 1.0, 0.0).astype(BF16)
    weighted = which * values_ref[...]
    v1 = weighted.astype(BF16)
    v2, v3 = split(weighted - v1.astype(F32))
    d = functools.partial(lax.dot_general, dimension_numbers=NT, preferred_element_type=F32)
    cnt_ref[...] = d(which.astype(BF16), slot)
    sum_ref[...] = d(v1, slot) + (d(v2, slot) + d(v3, slot))
    wi = lax.broadcasted_iota(jnp.int32, (WIN, 128), 0)
    window = jnp.zeros((WIN, 128), F32)
    for w in range(WIN):
        window = jnp.where(wi == w, par_ref[jnp.clip(base + w, 0, count - 1)], window)
    pw_ref[...] = window

    def window(k):
        return source_window(k, reg_ref, pat_ref, base, scale)

    for ref, at in ((xa, 0), (xb, half)):
        ref[0, :B, :] = low[at].T
        ref[0, B:, :] = window(at)
    for k in range(1, half):
        a = advance(xa[k - 1], low[k])
        b = advance(xb[k - 1], low[k + half])
        xa[k, :B, :] = a[:B]
        xa[k, B:, :] = a[B:] + window(k)
        xb[k, :B, :] = b[:B]
        xb[k, B:, :] = b[B:] + window(k + half)
        if k == 2:
            for i in range(blocks):
                copy(i).wait()
        if k >= 2:
            z_ref[k - 2] = dot3(xa[k - 2], piv[k - 2], NT)
    for k in range(half):
        full = advance(xa[half - 1], xb[k, :B, :], NN)
        full = jnp.concatenate([full[:B], full[B:] + xb[k, B:, :]], axis=0)
        if k < 2:
            z_ref[half - 2 + k] = dot3(xa[half - 2 + k], piv[half - 2 + k], NT)
        z_ref[half + k] = dot3(full, piv[half + k], NT)
    f_ref[...] = full[B:]


def lines_kernel(blocks, up, z_ref, dep_ref, y_ref, token_ref, parts):
    half = blocks // 2
    last = blocks - 1
    y_ref[last, :ROWS, :] = z_ref[last]
    y_ref[last, ROWS:, :] = up[last].T
    parts[half - 1, :ROWS, :] = z_ref[half - 1]
    parts[half - 1, ROWS:, :] = up[half - 1].T
    for k in range(half - 2, -1, -1):
        a = advance(y_ref[k + half + 1], up[k + half])
        b = advance(parts[k + 1], up[k])
        y_ref[k + half, :ROWS, :] = a[:ROWS] + z_ref[k + half]
        y_ref[k + half, ROWS:, :] = a[ROWS:]
        parts[k, :ROWS, :] = b[:ROWS] + z_ref[k]
        parts[k, ROWS:, :] = b[ROWS:]
    for k in range(half):
        full = advance(y_ref[half], parts[k, ROWS:, :], NN)
        y_ref[k, :ROWS, :] = full[:ROWS] + parts[k, :ROWS, :]
        y_ref[k, ROWS:, :] = full[ROWS:]
    token_ref[...] = jnp.zeros((8, 128), F32)


def line_kernel(own_ref, mine_ref, r1_ref, r2_ref, r3_ref, dep_ref, maps_ref, row_ref, tail_ref):
    y, x, core = place()
    p = jnp.where(core == 0, x, 3 - x)
    i = lax.broadcasted_iota(jnp.int32, (AUG, B), 0)
    j = lax.broadcasted_iota(jnp.int32, (AUG, B), 1)
    eye = jnp.where(i == j, 1.0, 0.0)
    r1, r2, r3 = r1_ref[...], r2_ref[...], r3_ref[...]
    maps_ref[4] = mine_ref[...]
    maps_ref[0] = jnp.where(p >= 1, r1, eye)
    maps_ref[1] = jnp.where(p >= 2, r2, eye)
    pre = affine(jnp.where(p >= 3, r3, eye), maps_ref[1])
    suf = affine(jnp.where(p <= 2, r3, eye), jnp.where(p <= 1, r2, eye))
    maps_ref[2] = affine(pre, maps_ref[0])
    maps_ref[3] = affine(suf, jnp.where(p <= 0, r1, eye))
    row_ref[...] = affine(affine(maps_ref[2], own_ref[...]), maps_ref[3])
    tail_ref[...] = row_ref[B : B + 8, :]


def entering_kernel(own_ref, maps_ref, y1_ref, y2_ref, t3_ref, dep_ref, chip_ref, next_ref):
    y, x, core = place()
    t1 = jnp.where(y >= 1, y1_ref[B : B + 1, :], 0.0)
    t2 = jnp.where(y >= 2, y2_ref[B : B + 1, :], 0.0)
    t3 = jnp.where(y >= 3, t3_ref[0:1, :], 0.0)
    row = t1 + apply(t2 + apply(t3, y2_ref[:B, :]), y1_ref[:B, :])
    chip = maps_ref[2, B : B + 1, :] + apply(row, maps_ref[2, :B, :])
    following = own_ref[B : B + 1, :] + apply(chip, own_ref[:B, :])
    chip_ref[...] = jnp.broadcast_to(chip, (8, B))
    next_ref[...] = jnp.broadcast_to(following, (8, B))


def start_kernel(chip_ref, got_ref, pw_ref, y_ref, near1_ref, maps_ref, mapso_ref, dep1_ref, dep2_ref, in_ref, out_ref):
    my_y, my_x, core = place()
    entering = jnp.where(core == 0, chip_ref[0:1, :], got_ref[0:1, :])
    vb = jnp.concatenate([spread(entering), pw_ref[...]], axis=0)
    in_ref[...] = vb
    v = jnp.concatenate(
        [
            jnp.sum(vb * y_ref[0, :ROWS, :128], axis=0, keepdims=True),
            jnp.sum(vb * y_ref[0, :ROWS, 128:], axis=0, keepdims=True),
        ],
        axis=1,
    )
    z1 = jnp.where(core == 1, apply(v, near1_ref[:B, :]), v)
    z2 = apply(z1, jnp.where(core == 1, maps_ref[3, :B, :], mapso_ref[3, :B, :]))
    ty, tx, tc = row_coords()
    same = ty == my_y
    scatter_rows(
        out_ref,
        [
            (same & (tx == my_x) & (tc < core), v),
            (same & (tx < my_x), z1),
            (ty < my_y, z2),
        ],
    )


class Maps:
    def __init__(self, core, side, near, maps, steps):
        self.mine = core == side
        self.near_ref, self.map_refs, self.step_refs = near, maps, steps

    def near(self):
        return jnp.where(self.mine, self.near_ref[:B, :], self.map_refs[1][4, :B, :])

    def line(self, i):
        return jnp.where(self.mine, self.map_refs[0][i, :B, :], self.map_refs[1][i, :B, :])

    def step(self, j):
        mine, other = self.step_refs[j - 1]
        return jnp.where(self.mine, mine[:B, :], other[:B, :])


def spread_out(out_ref, first, m, leftward):
    my_y, my_x, core = place()
    side = 1 if leftward else 0
    g = jnp.where(core == side, apply_t(first, m.near()), first)
    g2 = apply_t(g, m.line(0))
    g3 = apply_t(g2, m.line(1))
    h = apply_t(g, m.line(2))
    h2 = apply_t(h, m.step(1))
    h3 = apply_t(h2, m.step(2))
    ty, tx, tc = row_coords()
    sign = -1 if leftward else 1
    dy, dx, dc = sign * (ty - my_y), sign * (tx - my_x), sign * (tc - core)
    same = dy == 0
    scatter_rows(
        out_ref,
        [
            (same & (dx == 0) & (dc > 0), first),
            (same & (dx == 1), g),
            (same & (dx == 2), g2),
            (same & (dx == 3), g3),
            (dy == 1, h),
            (dy == 2, h2),
            (dy == 3, h3),
        ],
    )


def collect(got_ref, m, leftward):
    my_y, my_x, core = place()
    sy, sx, sc = row_coords()
    same = sy == my_y
    part, mx, my = gather_rows(got_ref, [same & (sx == my_x), same & (sx != my_x), sy != my_y])
    total = mx + apply_t(my, m.line(3))
    side = 0 if leftward else 1
    return part + jnp.where(core == side, apply_t(total, m.near()), total)


def middle_kernel(
    blocks, got_ref, got0_ref, maps_ref, mapso_ref, y1_ref, y1o_ref, y2_ref, y2o_ref,
    in_ref, y_ref, cnt_ref, sum_ref, sol_ref, out_ref, acc_ref, sb, acc_r
):
    my_y, my_x, core = place()
    m = Maps(core, 1, got0_ref, (maps_ref, mapso_ref), ((y1_ref, y1o_ref), (y2_ref, y2o_ref)))
    sy, sx, sc = row_coords()
    same = sy == my_y
    part, t1, t2, t3, y1, y2, y3 = gather_rows(
        got_ref,
        [same & (sx == my_x)]
        + [same & (sx == my_x + j) for j in (1, 2, 3)]
        + [sy == my_y + j for j in (1, 2, 3)],
    )
    yv = y1 + apply(y2 + apply(y3, m.step(2)), m.step(1))
    xv = t1 + apply(t2 + apply(t3, m.line(1)), m.line(0)) + apply(yv, m.line(2))
    entering = part + jnp.where(core == 0, apply(xv, m.near()), xv)
    sb[...] = spread(entering)
    acc_ref[...] = jnp.zeros((ROWS, 128), F32)
    acc_r[...] = jnp.zeros((B, 128), F32)

    for k in range(blocks):
        vb, wb = in_ref[...], sb[...]
        row = jnp.concatenate(
            [
                jnp.sum(vb * y_ref[k, :ROWS, half], axis=0, keepdims=True)
                + jnp.sum(wb * y_ref[k, ROWS:, half], axis=0, keepdims=True)
                for half in (slice(0, 128), slice(128, 256))
            ],
            axis=1,
        )
        sol_ref[k : k + 1, :] = row
        forcing = cnt_ref[k : k + 1, :] * row - sum_ref[k : k + 1, :]
        left, right = forcing[:, :128], forcing[:, 128:]
        acc_ref[...] += y_ref[k, :ROWS, :128] * left + y_ref[k, :ROWS, 128:] * right
        acc_r[...] += y_ref[k, ROWS:, :128] * left + y_ref[k, ROWS:, 128:] * right

    acc_ref[...] = jnp.broadcast_to(jnp.sum(acc_ref[...], axis=1, keepdims=True), (ROWS, 128))
    first = to_row(jnp.sum(acc_r[...], axis=1, keepdims=True))
    spread_out(out_ref, first, m, False)


def return_kernel(
    got_ref, got0_ref, maps_ref, mapso_ref, y1_ref, y1o_ref, y2_ref, y2o_ref, acc_ref, y_ref,
    out_ref, gw_ref
):
    core = place()[2]
    upper = Maps(core, 1, got0_ref, (maps_ref, mapso_ref), None)
    lower = Maps(core, 0, got0_ref, (maps_ref, mapso_ref), ((y1_ref, y1o_ref), (y2_ref, y2o_ref)))
    c_in = collect(got_ref, upper, False)
    column = acc_ref[:, 0:1] + adjoint_column(c_in, y_ref[0, :ROWS, :])
    gw_ref[...] = jnp.broadcast_to(column[B:], (WIN, 128))
    spread_out(out_ref, to_row(column[:B]), lower, True)


def window_kernel(blocks, regions, got_ref, got0_ref, maps_ref, mapso_ref, gw_ref, f_ref, out_ref):
    core = place()[2]
    base = window_base(blocks, regions)
    lower = Maps(core, 0, got0_ref, (maps_ref, mapso_ref), None)
    a_in = collect(got_ref, lower, True)
    column = gw_ref[:, 0:1] + adjoint_column(a_in, f_ref[...])
    w = lax.broadcasted_iota(jnp.int32, (WIN, 128), 0)
    lane = lax.broadcasted_iota(jnp.int32, (WIN, 128), 1)
    row = jnp.sum(jnp.where(((base + w) & 127) == lane, column, 0.0), axis=0, keepdims=True)
    out_ref[...] = jnp.broadcast_to(row.reshape(1, 1, 128), out_ref.shape)


def total_kernel(blocks, groups, regions, tracers, got_ref, out_ref):
    total = got_ref[0:32, 0, :]
    for t in range(1, tracers):
        total = total + got_ref[32 * t : 32 * t + 32, 0, :]
    d = lax.broadcasted_iota(jnp.int32, (32, 128), 0)
    lane = lax.broadcasted_iota(jnp.int32, (32, 128), 1)
    base = (d * (blocks * regions)) // groups - 3
    tile = (base + ((lane - base) & 127)) >> 7
    for t in range(out_ref.shape[1] // 128 + 1):
        lo, hi = 128 * t, min(128 * t + 128, out_ref.shape[1])
        if hi > lo:
            row = jnp.sum(jnp.where(tile == t, total, 0.0), axis=0, keepdims=True)
            out_ref[:, lo:hi] = row[:, : hi - lo]


def device(y, x, core):
    return ((y % 4) * 4 + x % 4) * 2 + core


def shards(
    factor_lower, factor_pivot, factor_upper, source_pattern, regions, params, obs_cells, obs_values
):
    low, piv, up = factor_lower[0], factor_pivot[0], factor_upper[0]
    pat = source_pattern[0]
    blocks = low.shape[0]
    tracers = lax.axis_size("tracer")
    groups = blocks * lax.axis_size("sub")
    regions_all = params.shape[0]
    scale = float(groups) ** (-1.5)
    def shape(*dims):
        return jax.ShapeDtypeStruct(dims, F32)

    def near(*dims):
        return pltpu.VMEM(dims, F32)

    def far(*arrays):
        return [pltpu.with_memory_space_constraint(a, pltpu.HBM) for a in arrays]

    def call(kernel, outs, ins, scratch=(), limit=8, flops=0, traffic=0, name=None):
        return pl.pallas_call(
            kernel,
            out_shape=outs,
            in_specs=ins,
            out_specs=jax.tree.map(lambda _: VM, outs),
            scratch_shapes=list(scratch),
            compiler_params=pltpu.CompilerParams(vmem_limit_bytes=limit * MIB),
            cost_estimate=pl.CostEstimate(flops=flops, bytes_accessed=traffic, transcendentals=0),
            name=name,
        )

    def swap(a):
        return lax.ppermute(a, "sub", [(d, d ^ 1) for d in range(32)])

    def along_x(a, j):
        pairs = [(device(y, x, 0), device(y, x + j, 0)) for y in range(4) for x in range(4)]
        pairs += [(device(y, x, 1), device(y, x - j, 1)) for y in range(4) for x in range(4)]
        return lax.ppermute(a, "sub", pairs)

    def along_y(a, j):
        pairs = [(device(y, x, 0), device(y + j, x, 0)) for y in range(4) for x in range(4)]
        pairs += [(device(y, x, 1), device(y - j, x, 1)) for y in range(4) for x in range(4)]
        return lax.ppermute(a, "sub", pairs)

    def exchange(a):
        return lax.all_to_all(a, "sub", 0, 0)

    block = (blocks, B, B)
    own, send, low_near, up_near = call(
        functools.partial(composites_kernel, blocks, scale),
        (shape(AUG, B), shape(AUG, B), near(*block), near(*block)),
        [HBM] * 4 + [SM],
        [
            pltpu.VMEM((blocks, B), F32), pltpu.VMEM((blocks, B), jnp.int32),
            pltpu.VMEM((blocks, B), F32), pltpu.VMEM((PARTS, AUG, B), F32), pltpu.VMEM((PARTS, B, B), F32),
            pltpu.SemaphoreType.DMA((2, blocks)), pltpu.SemaphoreType.DMA((3,)),
        ],
        limit=12, flops=6 * 2 * 16 * B**3, traffic=8 * MIB, name="composites",
    )(*far(low, up, pat, regions), params)
    got = swap(send)
    chip = call(chip_kernel, shape(AUG, B), [VM, VM], flops=6 * B**3, name="chip")(own, got)
    r1, r2, r3 = [along_x(chip, j) for j in (1, 2, 3)]
    zt, ft, cnt, osum, pw = call(
        functools.partial(prefixes_kernel, blocks, scale),
        (near(blocks, ROWS, B), near(WIN, B), near(blocks, B), near(blocks, B), near(WIN, 128)),
        [VM, HBM, VM, VM, SM, VM, VM, ANY],
        [
            pltpu.VMEM(block, F32), pltpu.VMEM((blocks // 2, ROWS, B), F32),
            pltpu.VMEM((blocks // 2, ROWS, B), F32), pltpu.SemaphoreType.DMA((blocks,)),
        ],
        limit=14, flops=6 * 2 * 16 * B**3, traffic=8 * MIB, name="prefixes",
    )(low_near, *far(piv), pat, regions, params, obs_cells, obs_values, chip)
    maps, row, tail = call(
        line_kernel, (shape(5, AUG, B), shape(AUG, B), shape(8, B)), [VM, VM, VM, VM, VM, ANY],
        flops=6 * 6 * B**3, name="line",
    )(chip, own, r1, r2, r3, cnt)
    y1, y2, y3 = along_y(row, 1), along_y(row, 2), along_y(tail, 3)
    maps_o = swap(maps)
    yt, token = call(
        functools.partial(lines_kernel, blocks),
        (near(blocks, ROWS + B, B), near(8, 128)),
        [VM, VM, ANY],
        [pltpu.VMEM((blocks // 2, ROWS + B, B), F32)],
        limit=12, flops=6 * 3 * 16 * B**3, traffic=8 * MIB, name="lines",
    )(up_near, zt, y3)
    chip_in, following = call(
        entering_kernel, (shape(8, B), shape(8, B)), [VM] * 5 + [ANY], name="entering"
    )(own, maps, y1, y2, y3, token)
    following = swap(following)
    y1_o, y2_o = [swap(a) for a in lax.optimization_barrier((y1, y2, token))[:2]]
    messages = shape(32, 2, 128)
    vb, sent = call(start_kernel, (near(ROWS, 128), messages), [VM] * 7 + [ANY] * 2, name="start")(
        chip_in, following, pw, yt, got, maps, maps_o, y1_o, y2_o
    )
    got_s = exchange(sent)
    sol, sent, acc = call(
        functools.partial(middle_kernel, blocks),
        (shape(blocks, B), messages, near(ROWS, 128)),
        [VM] * 12,
        [pltpu.VMEM((B, 128), F32), pltpu.VMEM((B, 128), F32)],
        name="middle",
    )(got_s, got, maps, maps_o, y1, y1_o, y2, y2_o, vb, yt, cnt, osum)
    got_c = exchange(sent)
    sent, gw = call(return_kernel, (messages, near(WIN, 128)), [VM] * 10, name="return")(
        got_c, got, maps, maps_o, y1, y1_o, y2, y2_o, acc, yt
    )
    got_a = exchange(sent)
    sent = call(
        functools.partial(window_kernel, blocks, regions_all), shape(32 * tracers, 1, 128), [VM] * 6, name="window"
    )(got_a, got, maps, maps_o, gw, ft)
    spread_windows = lax.all_to_all(sent, ("tracer", "sub"), 0, 0)
    gradient = call(
        functools.partial(total_kernel, blocks, groups, regions_all, tracers), shape(1, regions_all), [VM],
        name="total",
    )(spread_windows)
    return (gradient.reshape(regions_all), sol[None])


def solution(mesh):
    return jax.shard_map(
        shards,
        mesh=mesh,
        in_specs=(
            P("tracer", "sub", None, None),
            P("tracer", "sub", None, None),
            P("tracer", "sub", None, None),
            P("tracer", "sub", None),
            P("sub", None),
            P(),
            P("tracer", "sub"),
            P("tracer", "sub"),
        ),
        out_specs=(P(), P("tracer", "sub", None)),
        check_vma=False,
    )
```
